32 devices in a mesh: band: 16 (over z, y, x), head: 2 (over core).
Axes of the slice: x: 2, y: 2, z: 4, core: 2. Of those that a mesh axis runs over, the one named last changes fastest.
Arguments:
- grid_state: bfloat16 [65536, 100], P('band'), may hold values from -6 to 6
- hidden_state: bfloat16 [16384, 1024], P('band', 'head'), may hold values from -6 to 6
- encoder_sources: int32 [16384, 32], P('band'), may hold values from 0 to 12287, as said below
- encoder_counts: int32 [16384], P('band'), may hold values from 1 to 32
- decoder_sources: int32 [65536, 4], P('band'), may hold values from 0 to 16383, as said below
- decoder_counts: int32 [65536], P('band'), may hold values from 1 to 4
- encoder_keys: bfloat16 [100, 1024], P(None, 'head'), may hold values from -0.625 to 0.625
- encoder_values: bfloat16 [100, 1024], P(None, 'head'), may hold values from -0.625 to 0.625
- encoder_query: bfloat16 [1024, 1024], P(None, 'head'), may hold values from -0.1875 to 0.1875
- encoder_output: bfloat16 [1024, 1024], P('head'), may hold values from -0.1875 to 0.1875
- window_query: bfloat16 [1024, 1024], P(None, 'head'), may hold values from -0.1875 to 0.1875
- window_keys: bfloat16 [1024, 1024], P(None, 'head'), may hold values from -0.1875 to 0.1875
- window_values: bfloat16 [1024, 1024], P(None, 'head'), may hold values from -0.1875 to 0.1875
- window_output: bfloat16 [1024, 1024], P('head'), may hold values from -0.1875 to 0.1875
- feed_up: bfloat16 [1024, 4096], P(None, 'head'), may hold values from -0.1875 to 0.1875
- feed_down: bfloat16 [4096, 1024], P('head'), may hold values from -0.09375 to 0.09375
- decoder_query: bfloat16 [100, 1024], P(None, 'head'), may hold values from -0.625 to 0.625
- decoder_keys: bfloat16 [1024, 1024], P(None, 'head'), may hold values from -0.1875 to 0.1875
- decoder_values: bfloat16 [1024, 1024], P(None, 'head'), may hold values from -0.1875 to 0.1875
- decoder_output: bfloat16 [1024, 100], P('head'), may hold values from -0.1875 to 0.1875
Outputs:
- grid_next: bfloat16 [65536, 100], P(('band', 'head'))
- hidden_final: bfloat16 [16384, 1024], P('band', 'head')
The draws below stay inside these ranges and needn't reach their ends.
Inputs may be any that keep to these rules, and one draw needn't show every extreme that they name: Grid band c holds the grid points c * 4096 to (c + 1) * 4096 - 1 and hidden band c the hidden nodes c * 1024 to (c + 1) * 1024 - 1; slot e of hidden node n names the grid point (n // 1024 - 1) * 4096 + encoder_sources[n, e], which lies in a band that exists. Only the first encoder_counts[n] slots are edges. `decoder_sources`: every slot of grid point g names a hidden node of the bands g // 4096 - 1 to g // 4096 + 1 that exist. Only the first decoder_counts[g] slots are edges.
All inputs are finite; a program needn't handle non-finite values.
Results may differ from the reference program's by a relative error of at most 0.015.
Values may be sent and summed in bfloat16 or wider, within the bound.
No kernel may reach another device: no remote copies, remote signals or barrier semaphores. Data moves between devices by JAX's collectives and lax.ppermute only.
A program may use at most 320 MiB of HBM per device.

```python
import jax
import jax.numpy as jnp
from jax import lax

D = 1024
FFN = 4096
VARS = 100
HALF_WIN = 560
H_DEV = 1024
G_DEV = 4096
E_ENC = 32
E_DEC = 4
HEAD_DIM = 64
HIDDEN_SIZE = 16384
GRID = 65536
N_BAND = 16
N_HEAD = 2


def draw_encoder_sources(key, part):
    target_band = jnp.arange(HIDDEN_SIZE, dtype=jnp.int32) // H_DEV
    lowest = jnp.where(target_band == 0, G_DEV, 0).astype(jnp.int32)
    highest = jnp.where(target_band == N_BAND - 1, 2 * G_DEV, 3 * G_DEV).astype(jnp.int32)
    return jax.random.randint(jax.random.fold_in(key, 11), (HIDDEN_SIZE, E_ENC), lowest[:, None], highest[:, None], dtype=jnp.int32)


def draw_decoder_sources(key, part):
    target_band = jnp.arange(GRID, dtype=jnp.int32) // G_DEV
    lowest = jnp.maximum(target_band - 1, 0) * H_DEV
    highest = jnp.minimum((target_band + 2) * H_DEV, HIDDEN_SIZE)
    return jax.random.randint(jax.random.fold_in(key, 23), (GRID, E_DEC), lowest[:, None], highest[:, None], dtype=jnp.int32)


def touch_ends(entries, rng, least, high):
    spot = [jax.random.randint(jax.random.fold_in(rng, axis), (), 0, length) for axis, length in enumerate(entries.shape)]
    widest = entries.shape.index(max(entries.shape))
    neighbour = spot[:widest] + [(spot[widest] + 1) % entries.shape[widest]] + spot[widest + 1:]
    return entries.at[tuple(spot)].set(least).at[tuple(neighbour)].set(high)


def steps_of(stream_key, shape, shards, least, top_value):
    def one(dim, parts):
        steps = jax.random.uniform(jax.random.fold_in(jax.random.fold_in(stream_key, 6), dim), (parts,), jnp.float32, least / len(shards), top_value / len(shards))
        return jnp.repeat(jnp.exp(steps), shape[dim] // parts).reshape((-1,) + (1,) * (len(shape) - dim - 1))

    loudness = one(*shards[0])
    for cut in shards[1:]:
        loudness = loudness * one(*cut)
    return loudness


def normal_values(key, extent, width, reach, pieces=(), kind=jnp.bfloat16):
    drawn = jax.random.normal(key, extent, jnp.float32) * width
    if len(pieces) > 0:
        drawn = steps_of(key, extent, pieces, -0.22, 0.18) * drawn
    return jnp.clip(drawn, min=-reach, max=reach).astype(kind)


def setup_inputs(seed: int = 0) -> dict:
    key_list = jax.random.split(jax.random.key(seed), 21)
    return {
        "grid_state": normal_values(key_list[0], (GRID, VARS), 1.0, 6.0, ((0, 16),)),
        "hidden_state": normal_values(key_list[1], (HIDDEN_SIZE, D), 1.0, 6.0, ((0, 16), (1, 2))),
        "encoder_sources": draw_encoder_sources(jax.random.fold_in(key_list[20], 71), 0),
        "encoder_counts": touch_ends(jax.random.randint(key_list[3], (HIDDEN_SIZE,), 1, E_ENC + 1), jax.random.fold_in(key_list[3], 1), 1, E_ENC).astype(jnp.int32),
        "decoder_sources": draw_decoder_sources(jax.random.fold_in(key_list[20], 71), 0),
        "decoder_counts": touch_ends(jax.random.randint(key_list[5], (GRID,), 1, E_DEC + 1), jax.random.fold_in(key_list[5], 1), 1, E_DEC).astype(jnp.int32),
        "encoder_keys": normal_values(key_list[6], (VARS, D), VARS ** -0.5, 0.625, ((1, 2),)),
        "encoder_values": normal_values(key_list[7], (VARS, D), VARS ** -0.5, 0.625, ((1, 2),)),
        "encoder_query": normal_values(key_list[8], (D, D), D ** -0.5, 0.1875, ((1, 2),)),
        "encoder_output": normal_values(key_list[9], (D, D), D ** -0.5, 0.1875, ((0, 2),)),
        "window_query": normal_values(key_list[10], (D, D), D ** -0.5, 0.1875, ((1, 2),)),
        "window_keys": normal_values(key_list[11], (D, D), D ** -0.5, 0.1875, ((1, 2),)),
        "window_values": normal_values(key_list[12], (D, D), D ** -0.5, 0.1875, ((1, 2),)),
        "window_output": normal_values(key_list[13], (D, D), D ** -0.5, 0.1875, ((0, 2),)),
        "feed_up": normal_values(key_list[14], (D, FFN), D ** -0.5, 0.1875, ((1, 2),)),
        "feed_down": normal_values(key_list[15], (FFN, D), FFN ** -0.5, 0.09375, ((0, 2),)),
        "decoder_query": normal_values(key_list[16], (VARS, D), VARS ** -0.5, 0.625, ((1, 2),)),
        "decoder_keys": normal_values(key_list[17], (D, D), D ** -0.5, 0.1875, ((1, 2),)),
        "decoder_values": normal_values(key_list[18], (D, D), D ** -0.5, 0.1875, ((1, 2),)),
        "decoder_output": normal_values(key_list[19], (D, VARS), D ** -0.5, 0.1875, ((0, 2),)),
    }


EPSILON = 1e-05
NEGATIVE = -1e+30

def layer_norm(matrix):
    as_float = matrix.astype(jnp.float32)
    centred = as_float - lax.optimization_barrier(jnp.mean(as_float, axis=-1, keepdims=True))
    variance = lax.optimization_barrier(jnp.mean(centred * centred, axis=-1, keepdims=True))
    return (centred * lax.rsqrt(variance + EPSILON)).astype(jnp.bfloat16)

def project(matrix, weight):
    return jnp.dot(matrix, weight, preferred_element_type=jnp.float32).astype(jnp.bfloat16)

def softmax_weights(scores):
    powers = jnp.exp(scores)
    return (powers / lax.optimization_barrier(jnp.sum(powers, axis=-1, keepdims=True))).astype(jnp.bfloat16)

def edge_attention(query, keys, values, counts):
    row_count, slot_count, full_width = keys.shape
    head_count = full_width // HEAD_DIM
    query_heads = query.reshape(row_count, head_count, HEAD_DIM).astype(jnp.float32)
    key_heads = keys.reshape(row_count, slot_count, head_count, HEAD_DIM).astype(jnp.float32)
    value_heads = values.reshape(row_count, slot_count, head_count, HEAD_DIM).astype(jnp.float32)
    scores = jnp.einsum('rhd,rehd->rhe', query_heads, key_heads) * HEAD_DIM ** (-0.5)
    slot_live = jnp.arange(slot_count, dtype=jnp.int32)[None, None, :] < counts.astype(jnp.int32)[:, None, None]
    weights = softmax_weights(jnp.where(slot_live, scores, NEGATIVE))
    mixed = jnp.einsum('rhe,rehd->rhd', weights.astype(jnp.float32), value_heads)
    return mixed.reshape(row_count, full_width).astype(jnp.bfloat16)

def window_attention(query, keys, values, live):
    query_count, full_width = query.shape
    span_count = keys.shape[0]
    head_count = full_width // HEAD_DIM
    query_heads = query.reshape(query_count, head_count, HEAD_DIM).astype(jnp.float32)
    key_heads = keys.reshape(span_count, head_count, HEAD_DIM).astype(jnp.float32)
    value_heads = values.reshape(span_count, head_count, HEAD_DIM).astype(jnp.float32)
    scores = jnp.einsum('qhd,shd->hqs', query_heads, key_heads) * HEAD_DIM ** (-0.5)
    weights = softmax_weights(jnp.where(live[None], scores, NEGATIVE))
    mixed = jnp.einsum('hqs,shd->qhd', weights.astype(jnp.float32), value_heads)
    return mixed.reshape(query_count, full_width).astype(jnp.bfloat16)

def head_sum(mixed, weight):
    row_count = mixed.shape[0]
    group_width = mixed.shape[1] // N_HEAD
    left_side = mixed.reshape(row_count, N_HEAD, group_width).astype(jnp.float32)
    right_side = weight.reshape(N_HEAD, group_width, weight.shape[1]).astype(jnp.float32)
    partials = jnp.einsum('rgc,gcd->rgd', left_side, right_side).astype(jnp.bfloat16)
    return lax.optimization_barrier(jnp.sum(partials.astype(jnp.float32), axis=1))

def reference(grid_state, hidden_state, encoder_sources, encoder_counts, decoder_sources, decoder_counts, encoder_keys, encoder_values, encoder_query, encoder_output, window_query, window_keys, window_values, window_output, feed_up, feed_down, decoder_query, decoder_keys, decoder_values, decoder_output):
    grid_key = project(grid_state, encoder_keys)
    grid_value = project(grid_state, encoder_values)
    enc_query = project(layer_norm(hidden_state), encoder_query)
    node_band = (jnp.arange(HIDDEN_SIZE, dtype=jnp.int32) // H_DEV).astype(jnp.int32)
    band_base = ((node_band - 1) * G_DEV).astype(jnp.int32)
    encoder_global = (encoder_sources.astype(jnp.int32) + band_base[:, None]).astype(jnp.int32)

    def encode(item):
        block_query, block_sources, block_counts = item
        return edge_attention(block_query, jnp.take(grid_key, block_sources, axis=0), jnp.take(grid_value, block_sources, axis=0), block_counts)
    enc_mix = lax.map(encode, (enc_query.reshape(N_BAND, H_DEV, D), encoder_global.reshape(N_BAND, H_DEV, E_ENC), encoder_counts.reshape(N_BAND, H_DEV))).reshape(HIDDEN_SIZE, D)
    hidden_mid = (hidden_state.astype(jnp.float32) + head_sum(enc_mix, encoder_output)).astype(jnp.bfloat16)
    normed_mid = layer_norm(hidden_mid)
    win_query = project(normed_mid, window_query)
    win_key = project(normed_mid, window_keys)
    win_value = project(normed_mid, window_values)
    padded_key = jnp.pad(win_key, ((HALF_WIN, HALF_WIN), (0, 0)))
    padded_value = jnp.pad(win_value, ((HALF_WIN, HALF_WIN), (0, 0)))
    block_rows = min(512, H_DEV)
    span_rows = block_rows + 2 * HALF_WIN

    def attend(start):
        block_query = lax.dynamic_slice_in_dim(win_query, start, block_rows, 0)
        block_key = lax.dynamic_slice_in_dim(padded_key, start, span_rows, 0)
        block_value = lax.dynamic_slice_in_dim(padded_value, start, span_rows, 0)
        query_pos = start + jnp.arange(block_rows, dtype=jnp.int32)
        key_pos = start - HALF_WIN + jnp.arange(span_rows, dtype=jnp.int32)
        distance = jnp.abs(query_pos[:, None] - key_pos[None, :])
        live = (distance <= HALF_WIN) & (key_pos[None, :] >= 0) & (key_pos[None, :] < HIDDEN_SIZE)
        return window_attention(block_query, block_key, block_value, live)
    starts = (jnp.arange(HIDDEN_SIZE // block_rows, dtype=jnp.int32) * block_rows).astype(jnp.int32)
    win_mix = lax.map(attend, starts).reshape(HIDDEN_SIZE, D)
    hidden_att = (hidden_mid.astype(jnp.float32) + head_sum(win_mix, window_output)).astype(jnp.bfloat16)
    inner = jax.nn.gelu(jnp.dot(layer_norm(hidden_att), feed_up, preferred_element_type=jnp.float32), approximate=True).astype(jnp.bfloat16)
    hidden_final = (hidden_att.astype(jnp.float32) + head_sum(inner, feed_down)).astype(jnp.bfloat16)
    normed_final = layer_norm(hidden_final)
    dec_key = project(normed_final, decoder_keys)
    dec_value = project(normed_final, decoder_values)
    dec_query = project(grid_state, decoder_query)

    def decode(item):
        block_query, block_sources, block_counts = item
        return edge_attention(block_query, jnp.take(dec_key, block_sources, axis=0), jnp.take(dec_value, block_sources, axis=0), block_counts)
    dec_mix = lax.map(decode, (dec_query.reshape(N_BAND, G_DEV, D), decoder_sources.reshape(N_BAND, G_DEV, E_DEC), decoder_counts.reshape(N_BAND, G_DEV))).reshape(GRID, D)
    update = jnp.dot(dec_mix, decoder_output, preferred_element_type=jnp.float32)
    grid_next = (grid_state.astype(jnp.float32) + update).astype(jnp.bfloat16)
    return (grid_next, hidden_final)
```

```python
import functools
import math

import jax
import jax.numpy as jnp
from jax import lax
from jax.experimental import pallas as pl
from jax.experimental.pallas import tpu as pltpu
from jax.sharding import PartitionSpec as P

HALF_WIN = 560
HEAD_DIM = 64
LANES = 128
EPSILON = 1e-05
NEGATIVE = -1e30
SCALE = HEAD_DIM ** (-0.5) * math.log2(math.e)

bf16 = jnp.bfloat16
f32 = jnp.float32
ROWS_BY_ROWS = (((1,), (1,)), ((), ()))
VMEM = pl.BlockSpec(memory_space=pltpu.VMEM)
SMEM = pl.BlockSpec(memory_space=pltpu.SMEM)
BIG = pltpu.CompilerParams(vmem_limit_bytes=58 * 2**20)


def dot(a, b):
    return jnp.dot(a, b, preferred_element_type=f32)


def layer_norm(matrix):
    x = matrix.astype(f32)
    centred = x - jnp.mean(x, axis=-1, keepdims=True)
    variance = jnp.mean(centred * centred, axis=-1, keepdims=True)
    return (centred * lax.rsqrt(variance + EPSILON)).astype(bf16)


def low_lanes(shape):
    return lax.broadcasted_iota(jnp.int32, shape, len(shape) - 1) % LANES < HEAD_DIM


def query_kernel(state, wq_mine, wq_other, keys_mine, keys_other, out):
    normed = layer_norm(state[...])
    pairs = wq_mine.shape[1] // LANES
    for side, (wq, keys) in enumerate(((wq_mine, keys_mine), (wq_other, keys_other))):
        query = (dot(normed, wq[...])).astype(bf16)
        for pair in range(pairs):
            two = query[:, pair * LANES : (pair + 1) * LANES]
            low = low_lanes(two.shape)
            weight = keys[:, pair * LANES : (pair + 1) * LANES]
            for sub in range(2):
                one = jnp.where(low if sub == 0 else ~low, two, jnp.zeros_like(two))
                out[(side * pairs + pair) * 2 + sub] = (
                    lax.dot_general(one, weight, ROWS_BY_ROWS, preferred_element_type=f32) * SCALE
                )


GROUP = 8
CHAINS = 4


def encoder_kernel(
    info, sources, counts, query, own, prev_mine, prev_other, next_mine, next_other,
    values_mine, values_other, out_mine, out_other, state,
    result, table, *scratch,
):
    picked, mix = scratch[:-1], scratch[-1]
    core = info[0]
    grid_count, width = own.shape
    half = prev_mine.shape[0]
    heads, rows, _ = query.shape
    slots = sources.shape[0] // rows
    span = GROUP * slots
    table[...] = jnp.zeros_like(table)

    def fill(start, ref):
        table[pl.ds(pl.multiple_of(start, 8), ref.shape[0]), :width] = ref[...].astype(f32)

    fill(core * half, prev_mine)
    fill((1 - core) * half, prev_other)
    fill(grid_count, own)
    fill(2 * grid_count + core * half, next_mine)
    fill(2 * grid_count + (1 - core) * half, next_other)

    node = lax.broadcasted_iota(jnp.int32, (GROUP, span), 0)
    slot = lax.broadcasted_iota(jnp.int32, (GROUP, span), 1) - node * slots

    def step(index, carry):
        groups = [index * CHAINS + chain for chain in range(CHAINS)]
        starts = [pl.multiple_of(group * GROUP, GROUP) for group in groups]
        for group, rows_ref in zip(groups, picked):
            for s in range(span):
                rows_ref[s : s + 1, :] = table[pl.ds(sources[group * span + s], 1), :]
        grids = [ref[...].astype(bf16) for ref in picked]
        live = [(slot >= 0) & (slot < counts[pl.ds(start, GROUP), :]) for start in starts]
        queries = [
            query[:, pl.ds(start, GROUP), :].reshape(heads * GROUP, LANES).astype(bf16)
            for start in starts
        ]
        scores = [
            lax.dot_general(q, g, ROWS_BY_ROWS, preferred_element_type=f32)
            for q, g in zip(queries, grids)
        ]
        powers = [
            jnp.where(on[None], jnp.exp2(s.reshape(heads, GROUP, span)), 0.0).reshape(
                heads * GROUP, span
            )
            for s, on in zip(scores, live)
        ]
        weights = [(p * (1.0 / jnp.sum(p, -1, keepdims=True))).astype(bf16) for p in powers]
        mixed = [dot(w, g) for w, g in zip(weights, grids)]
        for start, m in zip(starts, mixed):
            mix[:, pl.ds(start, GROUP), :] = m.reshape(heads, GROUP, LANES)
        return carry

    lax.fori_loop(0, rows // (GROUP * CHAINS), step, 0)

    pairs = values_mine.shape[1] // LANES
    total = state[...].astype(f32)
    for side, (values, out) in enumerate(((values_mine, out_mine), (values_other, out_other))):
        parts = []
        for pair in range(pairs):
            weight = values[:, pair * LANES : (pair + 1) * LANES]
            low = low_lanes(weight.shape)
            both = jnp.concatenate(
                [jnp.where(low, weight, 0.0).astype(bf16), jnp.where(low, 0.0, weight).astype(bf16)], 0
            )
            head = (side * pairs + pair) * 2
            two = jnp.concatenate([mix[head].astype(bf16), mix[head + 1].astype(bf16)], 1)
            parts.append(dot(two, both).astype(bf16))
        total = total + dot(jnp.concatenate(parts, 1), out[...])
    result[...] = total.astype(bf16)


def window_kernel(
    info, own, partner, far, far_more, near,
    wq_mine, wq_other, wk_mine, wk_other, wv_mine, wv_other,
    result, query, key, value, bias,
):
    core, first, total = info[0], info[1], info[2]
    rows = own.shape[0]
    reach = HALF_WIN
    more = far_more.shape[0]
    lead = core == 0
    span_all = key.shape[1]
    pairs = wq_mine.shape[1] // LANES

    def put(target, start, block):
        for pair in range(pairs):
            target[0][target[1] * pairs + pair, pl.ds(pl.multiple_of(start, 16), block.shape[0]), :] = (
                block[:, pair * LANES : (pair + 1) * LANES]
            )

    segments = (
        (own, reach),
        (partner, jnp.where(lead, reach + rows, reach - rows)),
        (far, jnp.where(lead, more, reach + rows)),
        (far_more, jnp.where(lead, 0, reach + 2 * rows)),
        (near, jnp.where(lead, reach + 2 * rows, 0)),
    )
    for ref, start in segments:
        normed = layer_norm(ref[...])
        for side, (wk, wv) in enumerate(((wk_mine, wv_mine), (wk_other, wv_other))):
            put((key, side), start, dot(normed, wk[...]).astype(bf16))
            put((value, side), start, dot(normed, wv[...]).astype(bf16))
        if ref is own:
            for side, wq in enumerate((wq_mine, wq_other)):
                put((query, side), 0, (dot(normed, wq[...]).astype(bf16).astype(f32) * SCALE).astype(bf16))

    blocks, block, span = bias.shape
    for b in range(blocks):
        row = lax.broadcasted_iota(jnp.int32, (block, span), 0)
        col = lax.broadcasted_iota(jnp.int32, (block, span), 1)
        place = first - reach + b * block + col
        live = (col >= row) & (col <= row + 2 * reach) & (place >= 0) & (place < total)
        bias[b] = jnp.where(live, 0.0, NEGATIVE)

    def step(pair, carry):
        for b in range(blocks):
            k = key[pair, pl.ds(b * block, span), :]
            v = value[pair, pl.ds(b * block, span), :]
            q = query[pair, pl.ds(b * block, block), :]
            low = low_lanes(q.shape)
            mixes = []
            for sub in range(2):
                one = jnp.where(low if sub == 0 else ~low, q, jnp.zeros_like(q))
                s = lax.dot_general(one, k, ROWS_BY_ROWS, preferred_element_type=f32)
                p = jnp.exp2(s + bias[b])
                w = (p * (1.0 / jnp.sum(p, -1, keepdims=True))).astype(bf16)
                mixes.append(dot(w, v))
            result[pair, pl.ds(b * block, block), :] = jnp.where(low, mixes[0], mixes[1]).astype(bf16)
        return carry

    lax.fori_loop(0, 2 * pairs, step, 0)


def feed_kernel(mix, mid, wo_mine, wo_other, up_mine, up_other, down_mine, down_other, result, att, normed, total):
    index = pl.program_id(0)
    half = pl.num_programs(0) // 2

    @pl.when(index == 0)
    def _():
        pairs = wo_mine.shape[0] // LANES
        acc = mid[...].astype(f32)
        for side, wo in enumerate((wo_mine, wo_other)):
            block = jnp.concatenate([mix[side * pairs + pair] for pair in range(pairs)], 1)
            acc = acc + dot(block, wo[...])
        att[...] = acc.astype(bf16)
        normed[...] = layer_norm(att[...])
        total[...] = att[...].astype(f32)

    def part(up, down):
        inner = jax.nn.gelu(dot(normed[...], up[...]), approximate=True).astype(bf16)
        total[...] += dot(inner, down[...])

    @pl.when(index < half)
    def _():
        part(up_mine, down_mine)

    @pl.when(index >= half)
    def _():
        part(up_other, down_other)

    @pl.when(index == 2 * half - 1)
    def _():
        result[...] = total[...].astype(bf16)


POINTS = 32


def decoder_kernel(
    info, sources, counts, grid, own, partner, prev_mine, prev_other, next_mine, next_other,
    wq_mine, wq_other, wk_mine, wk_other, wv_mine, wv_other, wo_mine, wo_other,
    result, table, query, product,
):
    core = info[0]
    rows = own.shape[0]
    nodes = 2 * rows
    parts = wk_mine.shape[1] // LANES
    deep = 2 * parts
    points = grid.shape[0]
    slots = sources.shape[0] // points
    piece = rows // 2

    starts = (
        (prev_mine, core * rows),
        (prev_other, (1 - core) * rows),
        (own, nodes + core * rows),
        (partner, nodes + (1 - core) * rows),
        (next_mine, 2 * nodes + core * rows),
        (next_other, 2 * nodes + (1 - core) * rows),
    )
    for ref, start in starts:

        def fill(index, carry, ref=ref, start=start):
            normed = layer_norm(ref[pl.ds(pl.multiple_of(index * piece, piece), piece), :])
            base = (start + index * piece) * (2 * deep)
            for group, weight in enumerate((wk_mine, wk_other, wv_mine, wv_other)):
                block = dot(normed, weight[...])
                for part in range(parts):
                    table[pl.ds(base + group * parts + part, piece, stride=2 * deep), :] = block[
                        :, part * LANES : (part + 1) * LANES
                    ]
            return carry

        lax.fori_loop(0, rows // piece, fill, 0)

    def ask(index, carry):
        own_grid = grid[pl.ds(pl.multiple_of(index * piece, piece), piece), :]
        for group, weight in enumerate((wq_mine, wq_other)):
            block = dot(own_grid, weight[...]) * SCALE
            for part in range(parts):
                query[pl.ds(index * (piece * deep) + group * parts + part, piece, stride=deep), :] = block[
                    :, part * LANES : (part + 1) * LANES
                ]
        return carry

    lax.fori_loop(0, points // piece, ask, 0)

    ones_row = lax.broadcasted_iota(jnp.int32, (2 * LANES, 2 * LANES), 0) // HEAD_DIM
    ones_col = lax.broadcasted_iota(jnp.int32, (2 * LANES, 2 * LANES), 1) // HEAD_DIM
    same_head = jnp.where(ones_row == ones_col, 1.0, 0.0).astype(bf16)
    half = POINTS * deep // 2

    def step(index, carry):
        first = index * POINTS
        for point in range(0, POINTS, 2):
            q = [query[pl.ds(pl.multiple_of((first + point + t) * deep, deep), deep), :] for t in range(2)]
            for slot in range(slots):
                terms = []
                for t in range(2):
                    at = pl.multiple_of(sources[(first + point + t) * slots + slot], deep)
                    terms.append(table[pl.ds(at, deep), :] * q[t])
                product[slot, point * deep : (point + 2) * deep, :] = jnp.concatenate(terms, 0).astype(bf16)
        live = jnp.concatenate(
            [jnp.full((deep, LANES), counts[first + point], jnp.int32) for point in range(POINTS)], 0
        )
        powers = []
        for slot in range(slots):
            wide = jnp.concatenate([product[slot, :half, :], product[slot, half:, :]], 1)
            score = dot(wide, same_head)
            score = jnp.concatenate([score[:, :LANES], score[:, LANES:]], 0)
            powers.append(jnp.where(live > slot, jnp.exp2(score), 0.0))
        total = powers[0]
        for slot in range(1, slots):
            total = total + powers[slot]
        inverse = 1.0 / total
        weights = [p * inverse for p in powers]
        for point in range(POINTS):
            mixed = None
            for slot in range(slots):
                at = pl.multiple_of(sources[(first + point) * slots + slot], deep)
                term = weights[slot][point * deep : (point + 1) * deep, :] * table[pl.ds(at + deep, deep), :]
                mixed = term if mixed is None else mixed + term
            query[pl.ds(pl.multiple_of((first + point) * deep, deep), deep), :] = mixed
        return carry

    lax.fori_loop(0, points // POINTS, step, 0)

    width = result.shape[1]

    def finish(index, carry):
        at = pl.ds(pl.multiple_of(index * piece, piece), piece)
        acc = None
        for group, weight in enumerate((wo_mine, wo_other)):
            block = jnp.concatenate(
                [
                    query[pl.ds(index * (piece * deep) + group * parts + part, piece, stride=deep), :].astype(bf16)
                    for part in range(parts)
                ],
                1,
            )
            term = dot(block, weight[...])
            acc = term if acc is None else acc + term
        result[at, :] = (grid[at, :].astype(f32)[:, :width] + acc[:, :width]).astype(bf16)
        return carry

    lax.fori_loop(0, points // piece, finish, 0)


def local(
    grid_state,
    hidden_state,
    encoder_sources,
    encoder_counts,
    decoder_sources,
    decoder_counts,
    encoder_keys,
    encoder_values,
    encoder_query,
    encoder_output,
    window_query,
    window_keys,
    window_values,
    window_output,
    feed_up,
    feed_down,
    decoder_query,
    decoder_keys,
    decoder_values,
    decoder_output,
):
    bands, band, core = lax.axis_size("band"), lax.axis_index("band"), lax.axis_index("head")
    cores = lax.axis_size("head")
    grid_count, width = grid_state.shape
    nodes, channels = hidden_state.shape
    rows, points = nodes // cores, grid_count // cores
    full = channels * cores
    heads = full // HEAD_DIM

    def swap(x):
        return lax.ppermute(x, "head", [(0, 1), (1, 0)])

    def onward(x):
        return lax.ppermute(x, "band", [(i, i + 1) for i in range(bands - 1)])

    def backward(x):
        return lax.ppermute(x, "band", [(i + 1, i) for i in range(bands - 1)])

    def my_part(x, size):
        return lax.dynamic_slice_in_dim(x, core * size, size, 0)

    def wide(x):
        return jnp.pad(x, ((0, LANES - x.shape[0]), (0, 0)))

    info = jnp.stack([core, band * nodes + core * rows, bands * nodes]).astype(jnp.int32)

    my_grid = my_part(grid_state, points)
    prev_mine, next_mine = onward(my_grid), backward(my_grid)
    prev_other, next_other = swap(prev_mine), swap(next_mine)

    kept = my_part(hidden_state, rows)
    got = swap(lax.dynamic_slice_in_dim(hidden_state, (1 - core) * rows, rows, 0))
    state = jnp.where(
        core == 0, jnp.concatenate([kept, got], 1), jnp.concatenate([got, kept], 1)
    )

    ek_mine, ev_mine, dq_mine = wide(encoder_keys), wide(encoder_values), wide(decoder_query)
    do_mine = jnp.pad(decoder_output, ((0, 0), (0, LANES - width)))

    query = pl.pallas_call(
        query_kernel,
        out_shape=jax.ShapeDtypeStruct((heads, rows, LANES), f32),
        in_specs=[VMEM] * 5,
        out_specs=VMEM,
        compiler_params=BIG,
        name="queries",
    )(state, encoder_query, swap(encoder_query), ek_mine, swap(ek_mine))

    my_sources = my_part(encoder_sources, rows).reshape(-1)
    my_counts = my_part(encoder_counts, rows)[:, None]
    slots = encoder_sources.shape[1]
    mid = pl.pallas_call(
        encoder_kernel,
        out_shape=jax.ShapeDtypeStruct((rows, full), bf16),
        in_specs=[SMEM, SMEM] + [VMEM] * 12,
        out_specs=VMEM,
        scratch_shapes=[pltpu.VMEM((3 * grid_count, LANES), f32)]
        + [pltpu.VMEM((GROUP * slots, LANES), f32) for _ in range(CHAINS)]
        + [pltpu.VMEM((heads, rows, LANES), f32)],
        compiler_params=BIG,
        name="encoder",
    )(
        info, my_sources, my_counts, query, grid_state, prev_mine, prev_other, next_mine, next_other,
        ev_mine, swap(ev_mine), encoder_output, swap(encoder_output), state,
    )

    more = HALF_WIN - rows
    partner = swap(mid)
    facing = [(2 * i + 1, 2 * i + 2) for i in range(bands - 1)]
    far = lax.ppermute(mid, ("band", "head"), facing + [(b, a) for a, b in facing])
    edge = jnp.where(core == 0, mid[rows - more :], mid[:more])
    far_more = lax.ppermute(
        edge,
        ("band", "head"),
        [(2 * i, 2 * i + 2) for i in range(bands - 1)] + [(2 * i + 3, 2 * i + 1) for i in range(bands - 1)],
    )
    near = swap(jnp.where(core == 0, far[rows - more :], far[:more]))

    block = rows // 2
    span = block + 2 * HALF_WIN
    keys_all = rows + 2 * HALF_WIN
    pairs = full // LANES
    mix = pl.pallas_call(
        window_kernel,
        out_shape=jax.ShapeDtypeStruct((pairs, rows, LANES), bf16),
        in_specs=[SMEM] + [VMEM] * 11,
        out_specs=VMEM,
        scratch_shapes=[
            pltpu.VMEM((pairs, rows, LANES), bf16),
            pltpu.VMEM((pairs, keys_all, LANES), bf16),
            pltpu.VMEM((pairs, keys_all, LANES), bf16),
            pltpu.VMEM((rows // block, block, span), f32),
        ],
        compiler_params=BIG,
        name="window",
    )(
        info, mid, partner, far, far_more, near,
        window_query, swap(window_query), window_keys, swap(window_keys), window_values, swap(window_values),
    )

    units = feed_up.shape[1]
    chunk = min(512, units)
    steps = units // chunk
    whole = lambda shape: pl.BlockSpec(shape, lambda i: (0,) * len(shape))
    final = pl.pallas_call(
        feed_kernel,
        grid=(2 * steps,),
        out_shape=jax.ShapeDtypeStruct((rows, full), bf16),
        in_specs=[
            whole((pairs, rows, LANES)),
            whole((rows, full)),
            whole((channels, full)),
            whole((channels, full)),
            pl.BlockSpec((full, chunk), lambda i: (0, jnp.minimum(i, steps - 1))),
            pl.BlockSpec((full, chunk), lambda i: (0, jnp.maximum(i - steps, 0))),
            pl.BlockSpec((chunk, full), lambda i: (jnp.minimum(i, steps - 1), 0)),
            pl.BlockSpec((chunk, full), lambda i: (jnp.maximum(i - steps, 0), 0)),
        ],
        out_specs=whole((rows, full)),
        scratch_shapes=[
            pltpu.VMEM((rows, full), bf16),
            pltpu.VMEM((rows, full), bf16),
            pltpu.VMEM((rows, full), f32),
        ],
        compiler_params=BIG,
        name="feed",
    )(
        mix, mid, window_output, swap(window_output), feed_up, swap(feed_up), feed_down, swap(feed_down),
    )

    final_partner = swap(final)
    before, after = onward(final), backward(final)
    before_other, after_other = swap(before), swap(after)
    columns = lax.dynamic_slice_in_dim(final, core * channels, channels, 1)
    partner_columns = lax.dynamic_slice_in_dim(final_partner, core * channels, channels, 1)
    hidden_final = jnp.where(
        core == 0,
        jnp.concatenate([columns, partner_columns], 0),
        jnp.concatenate([partner_columns, columns], 0),
    )

    deep = full // LANES
    dec_sources = ((my_part(decoder_sources, points) - (band - 1) * nodes) * (2 * deep)).reshape(-1)
    dec_counts = my_part(decoder_counts, points)
    dec_slots = decoder_sources.shape[1]
    grid_wide = jnp.pad(my_grid, ((0, 0), (0, LANES - width)))
    grid_next = pl.pallas_call(
        decoder_kernel,
        out_shape=jax.ShapeDtypeStruct((points, width), bf16),
        in_specs=[SMEM] * 3 + [VMEM] * 15,
        out_specs=VMEM,
        scratch_shapes=[
            pltpu.VMEM((3 * nodes * 2 * deep, LANES), f32),
            pltpu.VMEM((points * deep, LANES), f32),
            pltpu.VMEM((dec_slots, POINTS * deep, LANES), bf16),
        ],
        compiler_params=BIG,
        name="decoder",
    )(
        info, dec_sources, dec_counts, grid_wide, final, final_partner,
        before, before_other, after, after_other,
        dq_mine, swap(dq_mine), decoder_keys, swap(decoder_keys), decoder_values, swap(decoder_values),
        do_mine, swap(do_mine),
    )
    return (grid_next, hidden_final)


def solution(mesh):
    in_specs = (
        P("band", None),
        P("band", "head"),
        P("band", None),
        P("band"),
        P("band", None),
        P("band"),
        P(None, "head"),
        P(None, "head"),
        P(None, "head"),
        P("head", None),
        P(None, "head"),
        P(None, "head"),
        P(None, "head"),
        P("head", None),
        P(None, "head"),
        P("head", None),
        P(None, "head"),
        P(None, "head"),
        P(None, "head"),
        P("head", None),
    )
    out_specs = (P(("band", "head"), None), P("band", "head"))
    return jax.shard_map(local, mesh=mesh, in_specs=in_specs, out_specs=out_specs, check_vma=False)
```

```python
import functools
import math

import jax
import jax.numpy as jnp
from jax import lax
from jax.experimental import pallas as pl
from jax.experimental.pallas import tpu as pltpu
from jax.sharding import PartitionSpec as P

HALF_WIN = 560
HEAD_DIM = 64
LANES = 128
EPSILON = 1e-05
NEGATIVE = -1e30
SCALE = HEAD_DIM ** (-0.5) * math.log2(math.e)

bf16 = jnp.bfloat16
f32 = jnp.float32
ROWS_BY_ROWS = (((1,), (1,)), ((), ()))
VMEM = pl.BlockSpec(memory_space=pltpu.VMEM)
SMEM = pl.BlockSpec(memory_space=pltpu.SMEM)
ANY = pl.BlockSpec(memory_space=pl.ANY)
BIG = pltpu.CompilerParams(vmem_limit_bytes=58 * 2**20)


def cost(flops):
    return pl.CostEstimate(flops=flops, bytes_accessed=flops // 256, transcendentals=0)


def dot(a, b):
    return jnp.dot(a, b, preferred_element_type=f32)


def layer_norm(matrix):
    x = matrix.astype(f32)
    centred = x - jnp.mean(x, axis=-1, keepdims=True)
    variance = jnp.mean(centred * centred, axis=-1, keepdims=True)
    return (centred * lax.rsqrt(variance + EPSILON)).astype(bf16)


def low_lanes(shape):
    return lax.broadcasted_iota(jnp.int32, shape, len(shape) - 1) % LANES < HEAD_DIM


def query_kernel(state, wq_mine, wq_other, keys_mine, keys_other, passing, *refs):
    out, passed = refs[-2:]
    del passing, passed
    normed = layer_norm(state[...])
    pairs = wq_mine.shape[1] // LANES
    for side, (wq, keys) in enumerate(((wq_mine, keys_mine), (wq_other, keys_other))):
        query = (dot(normed, wq[...])).astype(bf16)
        for pair in range(pairs):
            two = query[:, pair * LANES : (pair + 1) * LANES]
            low = low_lanes(two.shape)
            weight = keys[:, pair * LANES : (pair + 1) * LANES]
            for sub in range(2):
                one = jnp.where(low if sub == 0 else ~low, two, jnp.zeros_like(two))
                out[(side * pairs + pair) * 2 + sub] = (
                    lax.dot_general(one, weight, ROWS_BY_ROWS, preferred_element_type=f32) * SCALE
                )


GRID_CHUNKS = 2
ENCODER_CHUNKS = 1
GROUP = 8
CHAINS = 4


def encoder_kernel(
    info, sources, counts, query, own, *refs, spots, skip,
):
    near, refs = refs[: len(spots)], refs[len(spots) :]
    values_mine, values_other, out_mine, out_other, state, result, table = refs[:7]
    picked, mix = refs[7:-1], refs[-1]
    grid_count, width = own.shape
    heads = query.shape[0]
    rows = result.shape[0]
    slots = sources.shape[0] // query.shape[1]
    span = GROUP * slots
    table[...] = jnp.zeros_like(table)

    def fill(start, ref):
        table[pl.ds(pl.multiple_of(start, 8), ref.shape[0]), :width] = ref[...].astype(f32)

    fill(grid_count, own)
    for ref, (place, offset) in zip(near, spots):
        fill(info[place] + offset, ref)

    node = lax.broadcasted_iota(jnp.int32, (GROUP, span), 0)
    slot = lax.broadcasted_iota(jnp.int32, (GROUP, span), 1) - node * slots

    def step(index, carry):
        groups = [index * CHAINS + chain for chain in range(CHAINS)]
        starts = [pl.multiple_of(group * GROUP, GROUP) for group in groups]
        for group, rows_ref in zip(groups, picked):
            base = group * span + skip * slots
            for s in range(span):
                rows_ref[s : s + 1, :] = table[pl.ds(sources[base + s], 1), :]
        grids = [ref[...].astype(bf16) for ref in picked]
        live = [(slot >= 0) & (slot < counts[pl.ds(start + skip, GROUP), :]) for start in starts]
        queries = [
            query[:, pl.ds(start + skip, GROUP), :].reshape(heads * GROUP, LANES).astype(bf16)
            for start in starts
        ]
        scores = [
            lax.dot_general(q, g, ROWS_BY_ROWS, preferred_element_type=f32)
            for q, g in zip(queries, grids)
        ]
        powers = [
            jnp.where(on[None], jnp.exp2(s.reshape(heads, GROUP, span)), 0.0).reshape(
                heads * GROUP, span
            )
            for s, on in zip(scores, live)
        ]
        weights = [(p * (1.0 / jnp.sum(p, -1, keepdims=True))).astype(bf16) for p in powers]
        mixed = [dot(w, g) for w, g in zip(weights, grids)]
        for start, m in zip(starts, mixed):
            mix[:, pl.ds(start, GROUP), :] = m.reshape(heads, GROUP, LANES)
        return carry

    lax.fori_loop(0, rows // (GROUP * CHAINS), step, 0)

    pairs = values_mine.shape[1] // LANES
    total = state[skip : skip + rows, :].astype(f32)
    for side, (values, out) in enumerate(((values_mine, out_mine), (values_other, out_other))):
        parts = []
        for pair in range(pairs):
            weight = values[:, pair * LANES : (pair + 1) * LANES]
            low = low_lanes(weight.shape)
            both = jnp.concatenate(
                [jnp.where(low, weight, 0.0).astype(bf16), jnp.where(low, 0.0, weight).astype(bf16)], 0
            )
            head = (side * pairs + pair) * 2
            two = jnp.concatenate([mix[head].astype(bf16), mix[head + 1].astype(bf16)], 1)
            parts.append(dot(two, both).astype(bf16))
        total = total + dot(jnp.concatenate(parts, 1), out[...])
    result[...] = total.astype(bf16)


def lay(start, block, refs):
    for ref in refs:
        block[start : start + ref.shape[0], :] = layer_norm(ref[...])
        start += ref.shape[0]
    return start


def project_pairs(target, rows, weights, scale=None):
    for side, weight in enumerate(weights):
        block = dot(rows, weight[...]).astype(bf16)
        if scale is not None:
            block = (block.astype(f32) * scale).astype(bf16)
        pairs = weight.shape[1] // LANES
        for pair in range(pairs):
            target[side * pairs + pair] = block[:, pair * LANES : (pair + 1) * LANES]


def score_bound(query, key):
    row = lax.broadcasted_iota(jnp.int32, (LANES, LANES), 0) // HEAD_DIM
    col = lax.broadcasted_iota(jnp.int32, (LANES, LANES), 1) // HEAD_DIM
    same_head = jnp.where(row == col, 1.0, 0.0).astype(bf16)

    def longest(ref):
        most = None
        for pair in range(ref.shape[0]):
            x = ref[pair].astype(f32)
            found = jnp.max(dot((x * x).astype(bf16), same_head), axis=0, keepdims=True)
            most = found if most is None else jnp.maximum(most, found)
        return jnp.max(most)

    return longest(query) * longest(key) * 1.05


SAFE = 100.0


def attend(query, key, value, bias, block, finish, free=0):
    pairs, rows, _ = query.shape
    heads_at = lambda q, low, sub: jnp.where(low if sub == 0 else ~low, q, jnp.zeros_like(q))
    safe = score_bound(query, key) <= SAFE * SAFE

    def plain(pair, carry):
        k, v = key[pair], value[pair]
        low_v = low_lanes(v.shape)
        ones = jnp.ones_like(v)
        sides = [jnp.where(low_v, v, ones), jnp.where(low_v, ones, v)]
        for start in range(0, rows, block):
            at = slice(start, start + block)
            q = query[pair, at, :]
            low = low_lanes(q.shape)
            found = []
            for sub in range(2):
                s = lax.dot_general(heads_at(q, low, sub), k, ROWS_BY_ROWS, preferred_element_type=f32)
                p = jnp.exp2(s[:, free:] + bias[at, free:]).astype(bf16)
                if free:
                    p = jnp.concatenate([jnp.exp2(s[:, :free]).astype(bf16), p], 1)
                found.append(dot(p, sides[sub]))
            sums = pltpu.roll(jnp.where(low, found[1], found[0]), HEAD_DIM, 1)
            mixed = jnp.where(low, found[0], found[1]) * (1.0 / jnp.where(sums == 0.0, 1.0, sums))
            finish(pair, at, mixed, sums)
        return carry

    def careful(pair, carry):
        for start in range(0, rows, block):
            at = slice(start, start + block)
            q = query[pair, at, :]
            low = low_lanes(q.shape)
            mixes, sums = [], []
            for sub in range(2):
                s = lax.dot_general(
                    heads_at(q, low, sub), key[pair], ROWS_BY_ROWS, preferred_element_type=f32
                )
                p = jnp.exp2(s + bias[at, :])
                total = jnp.sum(p, -1, keepdims=True)
                w = (p * (1.0 / jnp.where(total == 0.0, 1.0, total))).astype(bf16)
                mixes.append(dot(w, value[pair]))
                sums.append(total)
            finish(pair, at, jnp.where(low, mixes[0], mixes[1]), jnp.where(low, sums[0], sums[1]))
        return carry

    @pl.when(safe)
    def _():
        lax.fori_loop(0, pairs, plain, 0)

    @pl.when(jnp.logical_not(safe))
    def _():
        lax.fori_loop(0, pairs, careful, 0)


def near_window_kernel(info, *refs):
    count = (len(refs) - 14) // 2
    nodes, weights = refs[: 2 * count], refs[2 * count : 2 * count + 6]
    query, mix, total, token, normed, key, value, bias = refs[2 * count + 6 :]
    lay(0, normed, nodes)
    rows = query.shape[1]
    project_pairs(query, normed[:rows, :], weights[:2], SCALE)
    project_pairs(key, normed[...], weights[2:4])
    project_pairs(value, normed[...], weights[4:])
    row = lax.broadcasted_iota(jnp.int32, bias.shape, 0)
    col = lax.broadcasted_iota(jnp.int32, bias.shape, 1)
    place = jnp.where(col < rows, col, col - rows + jnp.where(info[0] == 0, rows, -rows))
    bias[...] = jnp.where(jnp.abs(row - place) <= HALF_WIN, 0.0, NEGATIVE)
    token[...] = jnp.zeros_like(token)

    def finish(pair, at, mixed, sums):
        mix[pair, at, :] = mixed
        total[pair, at, :] = sums

    attend(query, key, value, bias, rows // 2, finish, free=rows)


def far_window_kernel(info, query, near_mix, near_total, *refs):
    count = len(refs) - 9
    nodes, weights = refs[:count], refs[count : count + 4]
    result, normed, key, value, bias = refs[count + 4 :]
    rows = query.shape[1]
    more = nodes[-1].shape[0]
    used = lay(0, normed, nodes)
    normed[used:, :] = jnp.zeros_like(normed[used:, :])
    project_pairs(key, normed[...], weights[:2])
    project_pairs(value, normed[...], weights[2:])
    first, whole, lead = info[1], info[2], info[0] == 0
    row = lax.broadcasted_iota(jnp.int32, bias.shape, 0)
    col = lax.broadcasted_iota(jnp.int32, bias.shape, 1)
    place = jnp.where(
        col < rows,
        col + jnp.where(lead, -rows, rows),
        jnp.where(
            col < rows + more,
            col - rows + jnp.where(lead, -rows - more, 2 * rows),
            col - rows - more + jnp.where(lead, 2 * rows, -rows - more),
        ),
    )
    live = (jnp.abs(row - place) <= HALF_WIN) & (first + place >= 0) & (first + place < whole) & (col < used)
    bias[...] = jnp.where(live, 0.0, NEGATIVE)

    def finish(pair, at, mixed, sums):
        near_sums = near_total[pair, at, :]
        inverse = 1.0 / (near_sums + sums)
        result[pair, at, :] = (near_mix[pair, at, :] * (near_sums * inverse) + mixed * (sums * inverse)).astype(bf16)

    attend(query, key, value, bias, rows, finish)


def feed_kernel(mix, mid, wo_mine, wo_other, up_mine, up_other, down_mine, down_other, result, att, normed, total):
    index = pl.program_id(0)
    half = pl.num_programs(0) // 2

    @pl.when(index == 0)
    def _():
        pairs = wo_mine.shape[0] // LANES
        acc = mid[...].astype(f32)
        for side, wo in enumerate((wo_mine, wo_other)):
            block = jnp.concatenate([mix[side * pairs + pair] for pair in range(pairs)], 1)
            acc = acc + dot(block, wo[...])
        att[...] = acc.astype(bf16)
        normed[...] = layer_norm(att[...])
        total[...] = att[...].astype(f32)

    def part(up, down):
        inner = jax.nn.gelu(dot(normed[...], up[...]), approximate=True).astype(bf16)
        total[...] += dot(inner, down[...])

    @pl.when(index < half)
    def _():
        part(up_mine, down_mine)

    @pl.when(index >= half)
    def _():
        part(up_other, down_other)

    @pl.when(index == 2 * half - 1)
    def _():
        result[...] = total[...].astype(bf16)


POINTS = 32
FEED_CHUNKS = 2


def decoder_kernel(info, sources, counts, grid, *refs, spots):
    nodes_in, refs = refs[: len(spots)], refs[len(spots) :]
    wq_mine, wq_other, wk_mine, wk_other, wv_mine, wv_other, wo_mine, wo_other = refs[:8]
    result, table, query, product, gathered = refs[8:]
    deep = query.shape[1]
    points = grid.shape[0]
    slots = sources.shape[0] // points
    piece = 256

    for ref, (place, offset) in zip(nodes_in, spots):
        gathered[pl.ds(pl.multiple_of(info[place] + offset, 16), ref.shape[0]), :] = ref[...]
    count = gathered.shape[0] // 6

    def fill(index, carry):
        at = pl.ds(pl.multiple_of(index * count, 16), count)
        normed = layer_norm(gathered[at, :])
        for side, pair in enumerate(((wk_mine, wk_other), (wv_mine, wv_other))):
            block = jnp.concatenate([dot(normed, weight[...]) for weight in pair], 1)
            table[at, side * deep : (side + 1) * deep, :] = block.reshape(count, deep, LANES)
        return carry

    lax.fori_loop(0, 6, fill, 0)

    def ask(index, carry):
        at = pl.ds(pl.multiple_of(index * piece, piece), piece)
        own_grid = grid[at, :]
        block = jnp.concatenate([dot(own_grid, weight[...]) for weight in (wq_mine, wq_other)], 1) * SCALE
        query[at] = block.reshape(piece, deep, LANES)
        return carry

    lax.fori_loop(0, points // piece, ask, 0)

    ones_row = lax.broadcasted_iota(jnp.int32, (2 * LANES, 2 * LANES), 0) // HEAD_DIM
    ones_col = lax.broadcasted_iota(jnp.int32, (2 * LANES, 2 * LANES), 1) // HEAD_DIM
    same_head = jnp.where(ones_row == ones_col, 1.0, 0.0).astype(bf16)
    half = POINTS * deep // 2

    def step(index, carry):
        first = index * POINTS
        for point in range(0, POINTS, 2):
            q = [query[first + point + t] for t in range(2)]
            for slot in range(slots):
                terms = []
                for t in range(2):
                    at = sources[(first + point + t) * slots + slot]
                    terms.append(table[at, :deep, :] * q[t])
                product[slot, point * deep : (point + 2) * deep, :] = jnp.concatenate(terms, 0).astype(bf16)
        live = jnp.concatenate(
            [jnp.full((deep, LANES), counts[first + point], jnp.int32) for point in range(POINTS)], 0
        )
        powers = []
        for slot in range(slots):
            pair = jnp.concatenate([product[slot, :half, :], product[slot, half:, :]], 1)
            score = dot(pair, same_head)
            score = jnp.concatenate([score[:, :LANES], score[:, LANES:]], 0)
            powers.append(jnp.where(live > slot, jnp.exp2(score), 0.0))
        total = powers[0]
        for slot in range(1, slots):
            total = total + powers[slot]
        inverse = 1.0 / total
        weights = [p * inverse for p in powers]
        for point in range(POINTS):
            mixed = None
            for slot in range(slots):
                at = sources[(first + point) * slots + slot]
                term = weights[slot][point * deep : (point + 1) * deep, :] * table[at, deep:, :]
                mixed = term if mixed is None else mixed + term
            query[first + point] = mixed
        return carry

    lax.fori_loop(0, points // POINTS, step, 0)

    width = result.shape[1]
    inner = deep * LANES // 2

    def finish(index, carry):
        at = pl.ds(pl.multiple_of(index * piece, piece), piece)
        block = query[at].reshape(piece, deep * LANES).astype(bf16)
        acc = dot(block[:, :inner], wo_mine[...]) + dot(block[:, inner:], wo_other[...])
        result[at, :] = (grid[at, :].astype(f32)[:, :width] + acc[:, :width]).astype(bf16)
        return carry

    lax.fori_loop(0, points // piece, finish, 0)


def local(
    grid_state,
    hidden_state,
    encoder_sources,
    encoder_counts,
    decoder_sources,
    decoder_counts,
    encoder_keys,
    encoder_values,
    encoder_query,
    encoder_output,
    window_query,
    window_keys,
    window_values,
    window_output,
    feed_up,
    feed_down,
    decoder_query,
    decoder_keys,
    decoder_values,
    decoder_output,
):
    bands, band, core = lax.axis_size("band"), lax.axis_index("band"), lax.axis_index("head")
    cores = lax.axis_size("head")
    grid_count, width = grid_state.shape
    nodes, channels = hidden_state.shape
    rows, points = nodes // cores, grid_count // cores
    full = channels * cores
    heads = full // HEAD_DIM

    def swap(x):
        return lax.ppermute(x, "head", [(0, 1), (1, 0)])

    def pair_swap(x):
        return lax.ppermute(x, "band", [(i, i ^ 1) for i in range(bands)])

    def pass_on(x):
        jumps = [(i, i + 2) for i in range(0, bands - 2, 2)] + [(i, i - 2) for i in range(3, bands, 2)]
        return lax.ppermute(x, "band", jumps)

    def my_part(x, size):
        return lax.dynamic_slice_in_dim(x, core * size, size, 0)

    def wide(x):
        return jnp.pad(x, ((0, LANES - x.shape[0]), (0, 0)))

    even = band % 2 == 0
    near_side = jnp.where(even, 2, 0)
    far_side = 2 - near_side
    info = jnp.stack(
        [
            core,
            band * nodes + core * rows,
            bands * nodes,
            near_side * grid_count + core * points,
            near_side * grid_count + (1 - core) * points,
            far_side * grid_count + core * points,
            far_side * grid_count + (1 - core) * points,
            nodes + core * rows,
            nodes + (1 - core) * rows,
            near_side * nodes + core * rows,
            near_side * nodes + (1 - core) * rows,
            far_side * nodes + core * rows,
            far_side * nodes + (1 - core) * rows,
        ]
    ).astype(jnp.int32)

    my_grid = my_part(grid_state, points)
    grid_cut = points // GRID_CHUNKS
    firsts = [pair_swap(my_grid[chunk * grid_cut : (chunk + 1) * grid_cut]) for chunk in range(GRID_CHUNKS)]

    kept = my_part(hidden_state, rows)
    got = swap(lax.dynamic_slice_in_dim(hidden_state, (1 - core) * rows, rows, 0))
    state = jnp.where(
        core == 0, jnp.concatenate([kept, got], 1), jnp.concatenate([got, kept], 1)
    )

    ek_mine, ev_mine, dq_mine = wide(encoder_keys), wide(encoder_values), wide(decoder_query)
    do_mine = jnp.pad(decoder_output, ((0, 0), (0, LANES - width)))

    my_sources = my_part(encoder_sources, rows).reshape(-1)
    my_counts = my_part(encoder_counts, rows)[:, None]
    dec_sources = (my_part(decoder_sources, points) - (band - 1) * nodes).reshape(-1)
    dec_counts = my_part(decoder_counts, points)
    grid_wide = jnp.pad(my_grid, ((0, 0), (0, LANES - width)))
    early = (info, my_sources, my_counts, dec_sources, dec_counts, grid_wide)

    query, last = pl.pallas_call(
        query_kernel,
        out_shape=(
            jax.ShapeDtypeStruct((heads, rows, LANES), f32),
            jax.ShapeDtypeStruct(firsts[-1].shape, bf16),
        ),
        in_specs=[VMEM] * 5 + [ANY] * (1 + len(early)),
        out_specs=(VMEM, ANY),
        input_output_aliases={5: 1},
        compiler_params=BIG,
        cost_estimate=cost(6 * rows * full * full),
        name="queries",
    )(state, encoder_query, swap(encoder_query), ek_mine, swap(ek_mine), firsts[-1], *early)

    grid_parts, grid_spots = [], []
    for chunk, first in enumerate(firsts[:-1] + [last]):
        second = pass_on(first)
        grid_parts += [first, swap(first), second, swap(second)]
        grid_spots += [(3 + side, chunk * grid_cut) for side in range(4)]

    slots = encoder_sources.shape[1]
    encoder_rows = rows // ENCODER_CHUNKS
    encoder_inputs = (ev_mine, swap(ev_mine), encoder_output, swap(encoder_output))

    def encode(index):
        at = slice(index * encoder_rows, (index + 1) * encoder_rows)
        return pl.pallas_call(
            functools.partial(encoder_kernel, spots=tuple(grid_spots), skip=index * encoder_rows),
            out_shape=jax.ShapeDtypeStruct((encoder_rows, full), bf16),
            in_specs=[SMEM, SMEM] + [VMEM] * (8 + len(grid_spots)),
            out_specs=VMEM,
            scratch_shapes=[pltpu.VMEM((3 * grid_count, LANES), f32)]
            + [pltpu.VMEM((GROUP * slots, LANES), f32) for _ in range(CHAINS)]
            + [pltpu.VMEM((heads, encoder_rows, LANES), f32)],
            compiler_params=BIG,
            cost_estimate=cost(16 * rows * full * full),
            name="encoder",
        )(info, my_sources, my_counts, query, grid_state, *grid_parts, *encoder_inputs, state)

    more = HALF_WIN - rows
    facing = [(2 * i + 1, 2 * i + 2) for i in range(bands - 1)]
    facing = facing + [(b, a) for a, b in facing]
    mids, partners, fars = [], [], []
    for index in range(ENCODER_CHUNKS):
        mids.append(encode(index))
        sent = mids[-1]
        if index == ENCODER_CHUNKS - 1:
            edge = swap(jnp.where(core == 0, mids[-1][encoder_rows - more :], mids[0][:more]))
            sent = jnp.concatenate([sent, edge], 0)
        fars.append(lax.ppermute(sent, ("band", "head"), facing))
        partners.append(swap(mids[-1]))

    pairs = full // LANES
    window_weights = (window_keys, swap(window_keys), window_values, swap(window_values))
    near_count = 2 * rows
    win_query, near_mix, near_sum, token = pl.pallas_call(
        near_window_kernel,
        out_shape=(
            jax.ShapeDtypeStruct((pairs, rows, LANES), bf16),
            jax.ShapeDtypeStruct((pairs, rows, LANES), f32),
            jax.ShapeDtypeStruct((pairs, rows, LANES), f32),
            jax.ShapeDtypeStruct((8, LANES), jnp.int32),
        ),
        in_specs=[SMEM] + [VMEM] * (2 * ENCODER_CHUNKS + 6),
        out_specs=(VMEM,) * 4,
        scratch_shapes=[
            pltpu.VMEM((near_count, full), bf16),
            pltpu.VMEM((pairs, near_count, LANES), bf16),
            pltpu.VMEM((pairs, near_count, LANES), bf16),
            pltpu.VMEM((rows, near_count), f32),
        ],
        compiler_params=BIG,
        cost_estimate=cost(1024),
        name="near_window",
    )(info, *mids, *partners, window_query, swap(window_query), *window_weights)

    near = swap(
        jnp.where(core + token[0, 0] == 0, fars[-1][encoder_rows - more : encoder_rows], fars[0][:more])
    )
    far_count = -(-(rows + 2 * more) // LANES) * LANES
    mix = pl.pallas_call(
        far_window_kernel,
        out_shape=jax.ShapeDtypeStruct((pairs, rows, LANES), bf16),
        in_specs=[SMEM] + [VMEM] * (3 + ENCODER_CHUNKS + 1 + 4),
        out_specs=VMEM,
        scratch_shapes=[
            pltpu.VMEM((far_count, full), bf16),
            pltpu.VMEM((pairs, far_count, LANES), bf16),
            pltpu.VMEM((pairs, far_count, LANES), bf16),
            pltpu.VMEM((rows, far_count), f32),
        ],
        compiler_params=BIG,
        cost_estimate=cost(20 * rows * full * full),
        name="far_window",
    )(info, win_query, near_mix, near_sum, *fars, near, *window_weights)

    units = feed_up.shape[1]
    chunk = min(512, units)
    steps = units // chunk
    whole = lambda shape: pl.BlockSpec(shape, lambda i: (0,) * len(shape))
    cut = rows // FEED_CHUNKS
    weights = (
        window_output, swap(window_output), feed_up, swap(feed_up), feed_down, swap(feed_down),
    )

    def feed(index):
        return pl.pallas_call(
            feed_kernel,
            grid=(2 * steps,),
            out_shape=jax.ShapeDtypeStruct((cut, full), bf16),
            in_specs=[
                pl.BlockSpec((pairs, cut, LANES), lambda i: (0, index, 0)),
                pl.BlockSpec((cut, full), lambda i: (index, 0)),
                whole((channels, full)),
                whole((channels, full)),
                pl.BlockSpec((full, chunk), lambda i: (0, jnp.minimum(i, steps - 1))),
                pl.BlockSpec((full, chunk), lambda i: (0, jnp.maximum(i - steps, 0))),
                pl.BlockSpec((chunk, full), lambda i: (jnp.minimum(i, steps - 1), 0)),
                pl.BlockSpec((chunk, full), lambda i: (jnp.maximum(i - steps, 0), 0)),
            ],
            out_specs=whole((cut, full)),
            scratch_shapes=[
                pltpu.VMEM((cut, full), bf16),
                pltpu.VMEM((cut, full), bf16),
                pltpu.VMEM((cut, full), f32),
            ],
            compiler_params=BIG,
            cost_estimate=cost(2 * cut * full * (full + 4 * units)),
            name="feed",
        )(mix, mids[0], *weights)

    node_parts, node_spots, own_parts, partner_parts = [], [], [], []
    for index in range(FEED_CHUNKS):
        final = feed(index)
        first = pair_swap(final)
        other = swap(final)
        second = pass_on(first)
        own_parts.append(final)
        partner_parts.append(other)
        node_parts += [final, other, first, swap(first), second, swap(second)]
        node_spots += [(7 + side, index * cut) for side in range(6)]

    deep = full // LANES
    decoder_weights = (decoder_keys, swap(decoder_keys), decoder_values, swap(decoder_values))

    def columns(parts):
        return jnp.concatenate(
            [lax.dynamic_slice_in_dim(part, core * channels, channels, 1) for part in parts], 0
        )

    own_columns, partner_columns = columns(own_parts), columns(partner_parts)
    hidden_final = jnp.where(
        core == 0,
        jnp.concatenate([own_columns, partner_columns], 0),
        jnp.concatenate([partner_columns, own_columns], 0),
    )

    dec_slots = decoder_sources.shape[1]
    grid_next = pl.pallas_call(
        functools.partial(decoder_kernel, spots=tuple(node_spots)),
        out_shape=jax.ShapeDtypeStruct((points, width), bf16),
        in_specs=[SMEM] * 3 + [VMEM] * (9 + len(node_spots)),
        out_specs=VMEM,
        scratch_shapes=[
            pltpu.VMEM((3 * nodes, 2 * deep, LANES), f32),
            pltpu.VMEM((points, deep, LANES), f32),
            pltpu.VMEM((dec_slots, POINTS * deep, LANES), bf16),
            pltpu.VMEM((3 * nodes, full), bf16),
        ],
        compiler_params=BIG,
        name="decoder",
    )(
        info, dec_sources, dec_counts, grid_wide, *node_parts,
        dq_mine, swap(dq_mine), *decoder_weights,
        do_mine, swap(do_mine),
    )
    return (grid_next, hidden_final)


def solution(mesh):
    in_specs = (
        P("band", None),
        P("band", "head"),
        P("band", None),
        P("band"),
        P("band", None),
        P("band"),
        P(None, "head"),
        P(None, "head"),
        P(None, "head"),
        P("head", None),
        P(None, "head"),
        P(None, "head"),
        P(None, "head"),
        P("head", None),
        P(None, "head"),
        P("head", None),
        P(None, "head"),
        P(None, "head"),
        P(None, "head"),
        P("head", None),
    )
    out_specs = (P(("band", "head"), None), P("band", "head"))
    return jax.shard_map(local, mesh=mesh, in_specs=in_specs, out_specs=out_specs, check_vma=False)
```

```python
import functools
import math

import jax
import jax.numpy as jnp
from jax import lax
from jax.experimental import pallas as pl
from jax.experimental.pallas import tpu as pltpu
from jax.sharding import PartitionSpec as P

HALF_WIN = 560
HEAD_DIM = 64
LANES = 128
EPSILON = 1e-05
NEGATIVE = -1e30
SCALE = HEAD_DIM ** (-0.5) * math.log2(math.e)

bf16 = jnp.bfloat16
f32 = jnp.float32
ROWS_BY_ROWS = (((1,), (1,)), ((), ()))
VMEM = pl.BlockSpec(memory_space=pltpu.VMEM)
SMEM = pl.BlockSpec(memory_space=pltpu.SMEM)
ANY = pl.BlockSpec(memory_space=pl.ANY)
BIG = pltpu.CompilerParams(vmem_limit_bytes=58 * 2**20)


def cost(flops):
    return pl.CostEstimate(flops=flops, bytes_accessed=flops // 256, transcendentals=0)


def dot(a, b):
    return jnp.dot(a, b, preferred_element_type=f32)


def layer_norm(matrix):
    x = matrix.astype(f32)
    centred = x - jnp.mean(x, axis=-1, keepdims=True)
    variance = jnp.mean(centred * centred, axis=-1, keepdims=True)
    return (centred * lax.rsqrt(variance + EPSILON)).astype(bf16)


def low_lanes(shape):
    return lax.broadcasted_iota(jnp.int32, shape, len(shape) - 1) % LANES < HEAD_DIM


def query_kernel(state, wq_mine, wq_other, keys_mine, keys_other, passing, *refs):
    out, passed = refs[-2:]
    del passing, passed
    normed = layer_norm(state[...])
    pairs = wq_mine.shape[1] // LANES
    for side, (wq, keys) in enumerate(((wq_mine, keys_mine), (wq_other, keys_other))):
        query = (dot(normed, wq[...])).astype(bf16)
        for pair in range(pairs):
            two = query[:, pair * LANES : (pair + 1) * LANES]
            low = low_lanes(two.shape)
            weight = keys[:, pair * LANES : (pair + 1) * LANES]
            for sub in range(2):
                one = jnp.where(low if sub == 0 else ~low, two, jnp.zeros_like(two))
                out[(side * pairs + pair) * 2 + sub] = (
                    lax.dot_general(one, weight, ROWS_BY_ROWS, preferred_element_type=f32) * SCALE
                ).astype(bf16)


GRID_CHUNKS = 2
GROUP = 8
CHAINS = 4


def encoder_kernel(
    info, sources, counts, query, own, *refs, spots,
):
    near, refs = refs[: len(spots)], refs[len(spots) :]
    values_mine, values_other, out_mine, out_other, state, result, normed, table = refs[:8]
    picked, mix = refs[8:-1], refs[-1]
    grid_count, width = own.shape
    heads = query.shape[0]
    rows = result.shape[0]
    slots = sources.shape[0] // query.shape[1]
    span = GROUP * slots
    table[...] = jnp.zeros_like(table)

    def fill(start, ref):
        table[pl.ds(pl.multiple_of(start, 8), ref.shape[0]), :width] = ref[...].astype(f32)

    fill(grid_count, own)
    for ref, (place, offset) in zip(near, spots):
        fill(info[place] + offset, ref)

    node = lax.broadcasted_iota(jnp.int32, (GROUP, span), 0)
    slot = lax.broadcasted_iota(jnp.int32, (GROUP, span), 1) - node * slots

    def step(index, carry):
        groups = [index * CHAINS + chain for chain in range(CHAINS)]
        starts = [pl.multiple_of(group * GROUP, GROUP) for group in groups]
        for group, rows_ref in zip(groups, picked):
            base = group * span
            for s in range(span):
                rows_ref[s : s + 1, :] = table[pl.ds(sources[base + s], 1), :]
        grids = [ref[...].astype(bf16) for ref in picked]
        live = [(slot >= 0) & (slot < counts[pl.ds(start, GROUP), :]) for start in starts]
        asked = query[:, pl.ds(pl.multiple_of(index * (CHAINS * GROUP), 16), CHAINS * GROUP), :].astype(f32)
        queries = [
            asked[:, chain * GROUP : (chain + 1) * GROUP, :].reshape(heads * GROUP, LANES).astype(bf16)
            for chain in range(CHAINS)
        ]
        scores = [
            lax.dot_general(q, g, ROWS_BY_ROWS, preferred_element_type=f32)
            for q, g in zip(queries, grids)
        ]
        powers = [
            jnp.where(on[None], jnp.exp2(s.reshape(heads, GROUP, span)), 0.0).reshape(
                heads * GROUP, span
            )
            for s, on in zip(scores, live)
        ]
        weights = [(p * (1.0 / jnp.sum(p, -1, keepdims=True))).astype(bf16) for p in powers]
        mixed = [dot(w, g) for w, g in zip(weights, grids)]
        for start, m in zip(starts, mixed):
            mix[:, pl.ds(start, GROUP), :] = m.reshape(heads, GROUP, LANES)
        return carry

    lax.fori_loop(0, rows // (GROUP * CHAINS), step, 0)

    pairs = values_mine.shape[1] // LANES
    total = state[...].astype(f32)
    for side, (values, out) in enumerate(((values_mine, out_mine), (values_other, out_other))):
        parts = []
        for pair in range(pairs):
            weight = values[:, pair * LANES : (pair + 1) * LANES]
            low = low_lanes(weight.shape)
            both = jnp.concatenate(
                [jnp.where(low, weight, 0.0).astype(bf16), jnp.where(low, 0.0, weight).astype(bf16)], 0
            )
            head = (side * pairs + pair) * 2
            two = jnp.concatenate([mix[head].astype(bf16), mix[head + 1].astype(bf16)], 1)
            parts.append(dot(two, both).astype(bf16))
        total = total + dot(jnp.concatenate(parts, 1), out[...])
    result[...] = total.astype(bf16)
    normed[...] = layer_norm(result[...])


def lay(start, block, refs):
    for ref in refs:
        block[start : start + ref.shape[0], :] = ref[...]
        start += ref.shape[0]
    return start


def project_pairs(target, rows, weights, scale=None):
    for side, weight in enumerate(weights):
        block = dot(rows, weight[...]).astype(bf16)
        if scale is not None:
            block = (block.astype(f32) * scale).astype(bf16)
        pairs = weight.shape[1] // LANES
        for pair in range(pairs):
            target[side * pairs + pair] = block[:, pair * LANES : (pair + 1) * LANES]


def score_bound(query, key):
    row = lax.broadcasted_iota(jnp.int32, (LANES, LANES), 0) // HEAD_DIM
    col = lax.broadcasted_iota(jnp.int32, (LANES, LANES), 1) // HEAD_DIM
    same_head = jnp.where(row == col, 1.0, 0.0).astype(bf16)

    def longest(ref):
        most = None
        for pair in range(ref.shape[0]):
            x = ref[pair].astype(f32)
            found = jnp.max(dot((x * x).astype(bf16), same_head), axis=0, keepdims=True)
            most = found if most is None else jnp.maximum(most, found)
        return jnp.max(most)

    return longest(query) * longest(key) * 1.05


SAFE = 100.0


def attend(query, key, value, bias, block, finish, free=0):
    pairs, rows, _ = query.shape
    heads_at = lambda q, low, sub: jnp.where(low if sub == 0 else ~low, q, jnp.zeros_like(q))
    safe = score_bound(query, key) <= SAFE * SAFE

    def plain(pair, carry):
        k, v = key[pair], value[pair]
        low_v = low_lanes(v.shape)
        ones = jnp.ones_like(v)
        sides = [jnp.where(low_v, v, ones), jnp.where(low_v, ones, v)]
        for start in range(0, rows, block):
            at = slice(start, start + block)
            q = query[pair, at, :]
            low = low_lanes(q.shape)
            found = []
            for sub in range(2):
                s = lax.dot_general(heads_at(q, low, sub), k, ROWS_BY_ROWS, preferred_element_type=f32)
                p = jnp.exp2(s[:, free:] + bias[at, free:]).astype(bf16)
                if free:
                    p = jnp.concatenate([jnp.exp2(s[:, :free]).astype(bf16), p], 1)
                found.append(dot(p, sides[sub]))
            sums = pltpu.roll(jnp.where(low, found[1], found[0]), HEAD_DIM, 1)
            mixed = jnp.where(low, found[0], found[1]) * (1.0 / jnp.where(sums == 0.0, 1.0, sums))
            finish(pair, at, mixed, sums)
        return carry

    def careful(pair, carry):
        for start in range(0, rows, block):
            at = slice(start, start + block)
            q = query[pair, at, :]
            low = low_lanes(q.shape)
            mixes, sums = [], []
            for sub in range(2):
                s = lax.dot_general(
                    heads_at(q, low, sub), key[pair], ROWS_BY_ROWS, preferred_element_type=f32
                )
                p = jnp.exp2(s + bias[at, :])
                total = jnp.sum(p, -1, keepdims=True)
                w = (p * (1.0 / jnp.where(total == 0.0, 1.0, total))).astype(bf16)
                mixes.append(dot(w, value[pair]))
                sums.append(total)
            finish(pair, at, jnp.where(low, mixes[0], mixes[1]), jnp.where(low, sums[0], sums[1]))
        return carry

    @pl.when(safe)
    def _():
        lax.fori_loop(0, pairs, plain, 0)

    @pl.when(jnp.logical_not(safe))
    def _():
        lax.fori_loop(0, pairs, careful, 0)


def near_window_kernel(info, *refs):
    count = (len(refs) - 14) // 2
    nodes, weights = refs[: 2 * count], refs[2 * count : 2 * count + 6]
    query, mix, total, token, normed, key, value, bias = refs[2 * count + 6 :]
    lay(0, normed, nodes)
    rows = query.shape[1]
    project_pairs(query, normed[:rows, :], weights[:2], SCALE)
    project_pairs(key, normed[...], weights[2:4])
    project_pairs(value, normed[...], weights[4:])
    row = lax.broadcasted_iota(jnp.int32, bias.shape, 0)
    col = lax.broadcasted_iota(jnp.int32, bias.shape, 1)
    place = jnp.where(col < rows, col, col - rows + jnp.where(info[0] == 0, rows, -rows))
    bias[...] = jnp.where(jnp.abs(row - place) <= HALF_WIN, 0.0, NEGATIVE)
    token[...] = jnp.zeros_like(token)

    def finish(pair, at, mixed, sums):
        mix[pair, at, :] = mixed
        total[pair, at, :] = sums

    attend(query, key, value, bias, rows // 2, finish, free=rows)


def far_window_kernel(info, query, near_mix, near_total, *refs):
    count = len(refs) - 9
    nodes, weights = refs[:count], refs[count : count + 4]
    result, normed, key, value, bias = refs[count + 4 :]
    rows = query.shape[1]
    more = nodes[-1].shape[0]
    used = lay(0, normed, nodes)
    normed[used:, :] = jnp.zeros_like(normed[used:, :])
    project_pairs(key, normed[...], weights[:2])
    project_pairs(value, normed[...], weights[2:])
    first, whole, lead = info[1], info[2], info[0] == 0
    row = lax.broadcasted_iota(jnp.int32, bias.shape, 0)
    col = lax.broadcasted_iota(jnp.int32, bias.shape, 1)
    place = jnp.where(
        col < rows,
        col + jnp.where(lead, -rows, rows),
        jnp.where(
            col < rows + more,
            col - rows + jnp.where(lead, -rows - more, 2 * rows),
            col - rows - more + jnp.where(lead, 2 * rows, -rows - more),
        ),
    )
    live = (jnp.abs(row - place) <= HALF_WIN) & (first + place >= 0) & (first + place < whole) & (col < used)
    bias[...] = jnp.where(live, 0.0, NEGATIVE)

    def finish(pair, at, mixed, sums):
        near_sums = near_total[pair, at, :]
        inverse = 1.0 / (near_sums + sums)
        result[pair, at, :] = (near_mix[pair, at, :] * (near_sums * inverse) + mixed * (sums * inverse)).astype(bf16)

    attend(query, key, value, bias, rows, finish)


def feed_kernel(mix, mid, wo_mine, wo_other, up_mine, up_other, down_mine, down_other, result, passed, att, normed, total, *, start):
    index = pl.program_id(0)
    half = pl.num_programs(0) // 2

    @pl.when(index == 0)
    def _():
        pairs = wo_mine.shape[0] // LANES
        at = slice(start, start + result.shape[0])
        acc = mid[at, :].astype(f32)
        for side, wo in enumerate((wo_mine, wo_other)):
            block = jnp.concatenate([mix[side * pairs + pair, at, :] for pair in range(pairs)], 1)
            acc = acc + dot(block, wo[...])
        att[...] = acc.astype(bf16)
        normed[...] = layer_norm(att[...])
        total[...] = att[...].astype(f32)

    def part(up, down):
        inner = jax.nn.gelu(dot(normed[...], up[...]), approximate=True).astype(bf16)
        total[...] += dot(inner, down[...])

    @pl.when(index < half)
    def _():
        part(up_mine, down_mine)

    @pl.when(index >= half)
    def _():
        part(up_other, down_other)

    @pl.when(index == 2 * half - 1)
    def _():
        result[...] = total[...].astype(bf16)
        passed[...] = layer_norm(result[...])


def hold_kernel(*refs):
    del refs


POINTS = 32


def decoder_kernel(info, sources, counts, grid, *refs, spots):
    nodes_in, refs = refs[: len(spots)], refs[len(spots) :]
    wq_mine, wq_other, wo_mine, wo_other = refs[0], refs[1], refs[6], refs[7]
    result, table, query, product, gathered, weights, arrived, loaded = refs[8:]
    deep = query.shape[1]
    points = grid.shape[0]
    slots = sources.shape[0] // points
    piece = 256

    copies = [
        pltpu.make_async_copy(
            ref, gathered.at[pl.ds(pl.multiple_of(info[place] + offset, 16), ref.shape[0])], arrived.at[index]
        )
        for index, (ref, (place, offset)) in enumerate(zip(nodes_in, spots))
    ] + [pltpu.make_async_copy(ref, weights.at[index], loaded.at[index]) for index, ref in enumerate(refs[2:6])]
    for copy in copies:
        copy.start()
    count = gathered.shape[0] // 6

    def fill(index, carry):
        at = pl.ds(pl.multiple_of(index * count, 16), count)
        normed = gathered[at, :]
        for side in range(2):
            block = jnp.concatenate([dot(normed, weights[2 * side + half]) for half in range(2)], 1)
            table[at, side * deep : (side + 1) * deep, :] = block.reshape(count, deep, LANES)
        return carry

    def ask(index, carry):
        at = pl.ds(pl.multiple_of(index * piece, piece), piece)
        own_grid = grid[at, :]
        block = jnp.concatenate([dot(own_grid, weight[...]) for weight in (wq_mine, wq_other)], 1) * SCALE
        query[at] = block.reshape(piece, deep, LANES)
        return carry

    lax.fori_loop(0, points // piece, ask, 0)
    for copy in copies:
        copy.wait()
    lax.fori_loop(0, 6, fill, 0)

    ones_row = lax.broadcasted_iota(jnp.int32, (2 * LANES, 2 * LANES), 0) // HEAD_DIM
    ones_col = lax.broadcasted_iota(jnp.int32, (2 * LANES, 2 * LANES), 1) // HEAD_DIM
    same_head = jnp.where(ones_row == ones_col, 1.0, 0.0).astype(bf16)
    half = POINTS * deep // 2
    vectors = table.reshape(table.shape[0] * 2 * deep, LANES)

    def step(index, carry):
        first = index * POINTS
        for point in range(0, POINTS, 2):
            q = [query[first + point + t] for t in range(2)]
            for slot in range(slots):
                terms = []
                for t in range(2):
                    at = pl.multiple_of(sources[(first + point + t) * slots + slot], deep)
                    terms.append(vectors[pl.ds(at, deep), :] * q[t])
                product[slot, point * deep : (point + 2) * deep, :] = jnp.concatenate(terms, 0).astype(bf16)
        live = jnp.concatenate(
            [jnp.full((deep, LANES), counts[first + point], jnp.int32) for point in range(POINTS)], 0
        )
        powers = []
        for slot in range(slots):
            pair = jnp.concatenate([product[slot, :half, :], product[slot, half:, :]], 1)
            score = dot(pair, same_head)
            score = jnp.concatenate([score[:, :LANES], score[:, LANES:]], 0)
            powers.append(jnp.where(live > slot, jnp.exp2(score), 0.0))
        total = powers[0]
        for slot in range(1, slots):
            total = total + powers[slot]
        inverse = 1.0 / total
        weights = [p * inverse for p in powers]
        for point in range(POINTS):
            mixed = None
            for slot in range(slots):
                at = pl.multiple_of(sources[(first + point) * slots + slot], deep)
                term = weights[slot][point * deep : (point + 1) * deep, :] * vectors[pl.ds(at + deep, deep), :]
                mixed = term if mixed is None else mixed + term
            query[first + point] = mixed
        return carry

    lax.fori_loop(0, points // POINTS, step, 0)

    width = result.shape[0]
    inner = deep * LANES // 2

    def finish(index, carry):
        at = pl.ds(pl.multiple_of(index * piece, piece), piece)
        block = query[at].reshape(piece, deep * LANES).astype(bf16)
        acc = dot(block[:, :inner], wo_mine[...]) + dot(block[:, inner:], wo_other[...])
        result[:, at] = (grid[at, :].astype(f32) + acc).T[:width, :].astype(bf16)
        return carry

    lax.fori_loop(0, points // piece, finish, 0)


def local(
    grid_state,
    hidden_state,
    encoder_sources,
    encoder_counts,
    decoder_sources,
    decoder_counts,
    encoder_keys,
    encoder_values,
    encoder_query,
    encoder_output,
    window_query,
    window_keys,
    window_values,
    window_output,
    feed_up,
    feed_down,
    decoder_query,
    decoder_keys,
    decoder_values,
    decoder_output,
):
    bands, band, core = lax.axis_size("band"), lax.axis_index("band"), lax.axis_index("head")
    cores = lax.axis_size("head")
    grid_count, width = grid_state.shape
    nodes, channels = hidden_state.shape
    rows, points = nodes // cores, grid_count // cores
    full = channels * cores
    heads = full // HEAD_DIM

    def swap(x):
        return lax.ppermute(x, "head", [(0, 1), (1, 0)])

    def pair_swap(x):
        return lax.ppermute(x, "band", [(i, i ^ 1) for i in range(bands)])

    def pass_on(x):
        jumps = [(i, i + 2) for i in range(0, bands - 2, 2)] + [(i, i - 2) for i in range(3, bands, 2)]
        return lax.ppermute(x, "band", jumps)

    def my_part(x, size):
        return lax.dynamic_slice_in_dim(x, core * size, size, 0)

    def wide(x):
        return jnp.pad(x, ((0, LANES - x.shape[0]), (0, 0)))

    even = band % 2 == 0
    near_side = jnp.where(even, 2, 0)
    far_side = 2 - near_side
    info = jnp.stack(
        [
            core,
            band * nodes + core * rows,
            bands * nodes,
            near_side * grid_count + core * points,
            near_side * grid_count + (1 - core) * points,
            far_side * grid_count + core * points,
            far_side * grid_count + (1 - core) * points,
            nodes + core * rows,
            nodes + (1 - core) * rows,
            near_side * nodes + core * rows,
            near_side * nodes + (1 - core) * rows,
            far_side * nodes + core * rows,
            far_side * nodes + (1 - core) * rows,
        ]
    ).astype(jnp.int32)

    my_grid = my_part(grid_state, points)
    grid_cut = points // GRID_CHUNKS
    firsts = [pair_swap(my_grid[chunk * grid_cut : (chunk + 1) * grid_cut]) for chunk in range(GRID_CHUNKS)]

    kept = my_part(hidden_state, rows)
    got = swap(lax.dynamic_slice_in_dim(hidden_state, (1 - core) * rows, rows, 0))
    state = jnp.where(
        core == 0, jnp.concatenate([kept, got], 1), jnp.concatenate([got, kept], 1)
    )

    ek_mine, ev_mine, dq_mine = wide(encoder_keys), wide(encoder_values), wide(decoder_query)
    do_mine = jnp.pad(decoder_output, ((0, 0), (0, LANES - width)))

    my_sources = my_part(encoder_sources, rows).reshape(-1)
    my_counts = my_part(encoder_counts, rows)[:, None]
    dec_sources = ((my_part(decoder_sources, points) - (band - 1) * nodes) * (2 * full // LANES)).reshape(-1)
    dec_counts = my_part(decoder_counts, points)
    grid_wide = jnp.pad(my_grid, ((0, 0), (0, LANES - width)))
    early = (info, my_sources, my_counts)

    query, last = pl.pallas_call(
        query_kernel,
        out_shape=(
            jax.ShapeDtypeStruct((heads, rows, LANES), bf16),
            jax.ShapeDtypeStruct(firsts[-1].shape, bf16),
        ),
        in_specs=[VMEM] * 5 + [ANY] * (1 + len(early)),
        out_specs=(VMEM, ANY),
        input_output_aliases={5: 1},
        compiler_params=BIG,
        cost_estimate=cost(6 * rows * full * full),
        name="queries",
    )(state, encoder_query, swap(encoder_query), ek_mine, swap(ek_mine), firsts[-1], *early)

    grid_parts, grid_spots = [], []
    for chunk, first in enumerate(firsts[:-1] + [last]):
        second = pass_on(first)
        grid_parts += [first, swap(first), second, swap(second)]
        grid_spots += [(3 + side, chunk * grid_cut) for side in range(4)]

    slots = encoder_sources.shape[1]
    mid, normed_mid = pl.pallas_call(
        functools.partial(encoder_kernel, spots=tuple(grid_spots)),
        out_shape=(jax.ShapeDtypeStruct((rows, full), bf16),) * 2,
        in_specs=[SMEM, SMEM] + [VMEM] * (8 + len(grid_spots)),
        out_specs=(VMEM, VMEM),
        scratch_shapes=[pltpu.VMEM((3 * grid_count, LANES), f32)]
        + [pltpu.VMEM((GROUP * slots, LANES), f32) for _ in range(CHAINS)]
        + [pltpu.VMEM((heads, rows, LANES), f32)],
        compiler_params=BIG,
        cost_estimate=cost(16 * rows * full * full),
        name="encoder",
    )(
        info, my_sources, my_counts, query, grid_state, *grid_parts,
        ev_mine, swap(ev_mine), encoder_output, swap(encoder_output), state,
    )

    more = HALF_WIN - rows
    facing = [(2 * i + 1, 2 * i + 2) for i in range(bands - 1)]
    facing = facing + [(b, a) for a, b in facing]
    partner = swap(normed_mid)
    edge = jnp.where(core == 0, partner[:more], partner[rows - more :])
    far = lax.ppermute(jnp.concatenate([normed_mid, edge], 0), ("band", "head"), facing)

    pairs = full // LANES
    window_weights = (window_keys, swap(window_keys), window_values, swap(window_values))
    near_count = 2 * rows
    win_query, near_mix, near_sum, token = pl.pallas_call(
        near_window_kernel,
        out_shape=(
            jax.ShapeDtypeStruct((pairs, rows, LANES), bf16),
            jax.ShapeDtypeStruct((pairs, rows, LANES), f32),
            jax.ShapeDtypeStruct((pairs, rows, LANES), f32),
            jax.ShapeDtypeStruct((8, LANES), jnp.int32),
        ),
        in_specs=[SMEM] + [VMEM] * 8,
        out_specs=(VMEM,) * 4,
        scratch_shapes=[
            pltpu.VMEM((near_count, full), bf16),
            pltpu.VMEM((pairs, near_count, LANES), bf16),
            pltpu.VMEM((pairs, near_count, LANES), bf16),
            pltpu.VMEM((rows, near_count), f32),
        ],
        compiler_params=BIG,
        cost_estimate=cost(1024),
        name="near_window",
    )(info, normed_mid, partner, window_query, swap(window_query), *window_weights)

    near = swap(
        jnp.where(core + token[0, 0] == 0, far[rows - more : rows], far[:more])
    )
    far_count = -(-(rows + 2 * more) // LANES) * LANES
    mix = pl.pallas_call(
        far_window_kernel,
        out_shape=jax.ShapeDtypeStruct((pairs, rows, LANES), bf16),
        in_specs=[SMEM] + [VMEM] * 9,
        out_specs=VMEM,
        scratch_shapes=[
            pltpu.VMEM((far_count, full), bf16),
            pltpu.VMEM((pairs, far_count, LANES), bf16),
            pltpu.VMEM((pairs, far_count, LANES), bf16),
            pltpu.VMEM((rows, far_count), f32),
        ],
        compiler_params=BIG,
        cost_estimate=cost(20 * rows * full * full),
        name="far_window",
    )(info, win_query, near_mix, near_sum, far, near, *window_weights)

    units = feed_up.shape[1]
    chunk = min(512, units)
    steps = units // chunk
    whole = lambda shape: pl.BlockSpec(shape, lambda i: (0,) * len(shape))
    cuts = (rows * 5 // 8, rows - rows * 5 // 8)
    weights = (
        window_output, swap(window_output), feed_up, swap(feed_up), feed_down, swap(feed_down),
    )

    def feed(start, cut):
        return pl.pallas_call(
            functools.partial(feed_kernel, start=start),
            grid=(2 * steps,),
            out_shape=(jax.ShapeDtypeStruct((cut, full), bf16),) * 2,
            in_specs=[
                whole((pairs, rows, LANES)),
                whole((rows, full)),
                whole((channels, full)),
                whole((channels, full)),
                pl.BlockSpec((full, chunk), lambda i: (0, jnp.minimum(i, steps - 1))),
                pl.BlockSpec((full, chunk), lambda i: (0, jnp.maximum(i - steps, 0))),
                pl.BlockSpec((chunk, full), lambda i: (jnp.minimum(i, steps - 1), 0)),
                pl.BlockSpec((chunk, full), lambda i: (jnp.maximum(i - steps, 0), 0)),
            ],
            out_specs=(whole((cut, full)),) * 2,
            scratch_shapes=[
                pltpu.VMEM((cut, full), bf16),
                pltpu.VMEM((cut, full), bf16),
                pltpu.VMEM((cut, full), f32),
            ],
            compiler_params=BIG,
            cost_estimate=cost(2 * cut * full * (full + 4 * units)),
            name="feed",
        )(mix, mid, *weights)

    node_parts, node_spots, own_parts, partner_parts = [], [], [], []
    firsts, seconds = [], []
    for index, cut in enumerate(cuts):
        start = sum(cuts[:index])
        final, normed = feed(start, cut)
        first = pair_swap(normed)
        firsts.append(first)
        if index < len(cuts) - 1:
            seconds.append(pass_on(first))
        own_parts.append(lax.dynamic_slice_in_dim(final, core * channels, channels, 1))
        partner_parts.append(swap(lax.dynamic_slice_in_dim(final, (1 - core) * channels, channels, 1)))
        node_parts += [normed, swap(normed)]
        node_spots += [(7 + side, start) for side in range(2)]

    deep = full // LANES
    decoder_weights = (decoder_keys, swap(decoder_keys), decoder_values, swap(decoder_values))

    own_columns, partner_columns = jnp.concatenate(own_parts, 0), jnp.concatenate(partner_parts, 0)
    hidden_final = jnp.where(
        core == 0,
        jnp.concatenate([own_columns, partner_columns], 0),
        jnp.concatenate([partner_columns, own_columns], 0),
    )

    dec_slots = decoder_sources.shape[1]
    firsts[-1] = pl.pallas_call(
        hold_kernel,
        out_shape=jax.ShapeDtypeStruct(firsts[-1].shape, bf16),
        in_specs=[ANY] * 4,
        out_specs=ANY,
        input_output_aliases={0: 0},
        name="hold",
    )(firsts[-1], dec_sources, dec_counts, grid_wide)
    for index, first in enumerate(firsts):
        second = pass_on(first) if index == len(cuts) - 1 else seconds[index]
        node_parts += [first, swap(first), second, swap(second)]
        node_spots += [(9 + side, sum(cuts[:index])) for side in range(4)]

    grid_next = pl.pallas_call(
        functools.partial(decoder_kernel, spots=tuple(node_spots)),
        out_shape=jax.ShapeDtypeStruct((width, points), bf16),
        in_specs=[SMEM] * 3 + [VMEM] + [ANY] * len(node_spots) + [VMEM] * 2 + [ANY] * 4 + [VMEM] * 2,
        out_specs=VMEM,
        scratch_shapes=[
            pltpu.VMEM((3 * nodes, 2 * deep, LANES), f32),
            pltpu.VMEM((points, deep, LANES), f32),
            pltpu.VMEM((dec_slots, POINTS * deep, LANES), bf16),
            pltpu.VMEM((3 * nodes, full), bf16),
            pltpu.VMEM((4,) + decoder_keys.shape, bf16),
            pltpu.SemaphoreType.DMA((len(node_spots),)),
            pltpu.SemaphoreType.DMA((4,)),
        ],
        compiler_params=BIG,
        name="decoder",
    )(
        info, dec_sources, dec_counts, grid_wide, *node_parts,
        dq_mine, swap(dq_mine), *decoder_weights,
        do_mine, swap(do_mine),
    )
    return (grid_next.T, hidden_final)


def solution(mesh):
    in_specs = (
        P("band", None),
        P("band", "head"),
        P("band", None),
        P("band"),
        P("band", None),
        P("band"),
        P(None, "head"),
        P(None, "head"),
        P(None, "head"),
        P("head", None),
        P(None, "head"),
        P(None, "head"),
        P(None, "head"),
        P("head", None),
        P(None, "head"),
        P("head", None),
        P(None, "head"),
        P(None, "head"),
        P(None, "head"),
        P("head", None),
    )
    out_specs = (P(("band", "head"), None), P("band", "head"))
    return jax.shard_map(local, mesh=mesh, in_specs=in_specs, out_specs=out_specs, check_vma=False)
```

```python
import functools
import math

import jax
import jax.numpy as jnp
from jax import lax
from jax.experimental import pallas as pl
from jax.experimental.pallas import tpu as pltpu
from jax.sharding import PartitionSpec as P

HALF_WIN = 560
HEAD_DIM = 64
LANES = 128
EPSILON = 1e-05
NEGATIVE = -1e30
SCALE = HEAD_DIM ** (-0.5) * math.log2(math.e)

bf16 = jnp.bfloat16
f32 = jnp.float32
ROWS_BY_ROWS = (((1,), (1,)), ((), ()))
VMEM = pl.BlockSpec(memory_space=pltpu.VMEM)
SMEM = pl.BlockSpec(memory_space=pltpu.SMEM)
ANY = pl.BlockSpec(memory_space=pl.ANY)
BIG = pltpu.CompilerParams(vmem_limit_bytes=58 * 2**20)


def cost(flops):
    return pl.CostEstimate(flops=flops, bytes_accessed=flops // 256, transcendentals=0)


def dot(a, b):
    return jnp.dot(a, b, preferred_element_type=f32)


def layer_norm(matrix):
    x = matrix.astype(f32)
    centred = x - jnp.mean(x, axis=-1, keepdims=True)
    variance = jnp.mean(centred * centred, axis=-1, keepdims=True)
    return (centred * lax.rsqrt(variance + EPSILON)).astype(bf16)


def low_lanes(shape):
    return lax.broadcasted_iota(jnp.int32, shape, len(shape) - 1) % LANES < HEAD_DIM


def query_kernel(state, wq_mine, wq_other, keys_mine, keys_other, passing, *refs):
    out, passed = refs[-2:]
    del passing, passed
    normed = layer_norm(state[...])
    pairs = wq_mine.shape[1] // LANES
    for side, (wq, keys) in enumerate(((wq_mine, keys_mine), (wq_other, keys_other))):
        query = (dot(normed, wq[...])).astype(bf16)
        for pair in range(pairs):
            two = query[:, pair * LANES : (pair + 1) * LANES]
            low = low_lanes(two.shape)
            weight = keys[:, pair * LANES : (pair + 1) * LANES]
            for sub in range(2):
                one = jnp.where(low if sub == 0 else ~low, two, jnp.zeros_like(two))
                out[(side * pairs + pair) * 2 + sub] = (
                    lax.dot_general(one, weight, ROWS_BY_ROWS, preferred_element_type=f32) * SCALE
                ).astype(bf16)


GRID_CHUNKS = 2
GROUP = 8
CHAINS = 8


def encoder_kernel(
    info, sources, counts, query, own, *refs, spots,
):
    near, refs = refs[: len(spots)], refs[len(spots) :]
    values_mine, values_other, out_mine, out_other, state, result, normed, table = refs[:8]
    picked, mix = refs[8:-1], refs[-1]
    grid_count, width = own.shape
    heads = query.shape[0]
    rows = result.shape[0]
    slots = sources.shape[0] // query.shape[1]
    span = GROUP * slots
    table[...] = jnp.zeros_like(table)

    def fill(start, ref):
        table[pl.ds(pl.multiple_of(start, 8), ref.shape[0]), :width] = ref[...].astype(f32)

    fill(grid_count, own)
    for ref, (place, offset) in zip(near, spots):
        fill(info[place] + offset, ref)

    node = lax.broadcasted_iota(jnp.int32, (GROUP, span), 0)
    slot = lax.broadcasted_iota(jnp.int32, (GROUP, span), 1) - node * slots

    def step(index, carry):
        groups = [index * CHAINS + chain for chain in range(CHAINS)]
        starts = [pl.multiple_of(group * GROUP, GROUP) for group in groups]
        for group, rows_ref in zip(groups, picked):
            base = group * span
            for s in range(span):
                rows_ref[s : s + 1, :] = table[pl.ds(sources[base + s], 1), :]
        grids = [ref[...].astype(bf16) for ref in picked]
        live = [(slot >= 0) & (slot < counts[pl.ds(start, GROUP), :]) for start in starts]
        asked = query[:, pl.ds(pl.multiple_of(index * (CHAINS * GROUP), 16), CHAINS * GROUP), :].astype(f32)
        queries = [
            asked[:, chain * GROUP : (chain + 1) * GROUP, :].reshape(heads * GROUP, LANES).astype(bf16)
            for chain in range(CHAINS)
        ]
        scores = [
            lax.dot_general(q, g, ROWS_BY_ROWS, preferred_element_type=f32)
            for q, g in zip(queries, grids)
        ]
        powers = [
            jnp.where(on[None], jnp.exp2(s.reshape(heads, GROUP, span)), 0.0).reshape(
                heads * GROUP, span
            )
            for s, on in zip(scores, live)
        ]
        weights = [(p * (1.0 / jnp.sum(p, -1, keepdims=True))).astype(bf16) for p in powers]
        mixed = [dot(w, g) for w, g in zip(weights, grids)]
        for start, m in zip(starts, mixed):
            mix[:, pl.ds(start, GROUP), :] = m.reshape(heads, GROUP, LANES)
        return carry

    lax.fori_loop(0, rows // (GROUP * CHAINS), step, 0)

    pairs = values_mine.shape[1] // LANES
    total = state[...].astype(f32)
    for side, (values, out) in enumerate(((values_mine, out_mine), (values_other, out_other))):
        parts = []
        for pair in range(pairs):
            weight = values[:, pair * LANES : (pair + 1) * LANES]
            low = low_lanes(weight.shape)
            both = jnp.concatenate(
                [jnp.where(low, weight, 0.0).astype(bf16), jnp.where(low, 0.0, weight).astype(bf16)], 0
            )
            head = (side * pairs + pair) * 2
            two = jnp.concatenate([mix[head].astype(bf16), mix[head + 1].astype(bf16)], 1)
            parts.append(dot(two, both).astype(bf16))
        total = total + dot(jnp.concatenate(parts, 1), out[...])
    result[...] = total.astype(bf16)
    normed[...] = layer_norm(result[...])


def lay(start, block, refs):
    for ref in refs:
        block[start : start + ref.shape[0], :] = ref[...]
        start += ref.shape[0]
    return start


def project_pairs(target, rows, weights, scale=None):
    for side, weight in enumerate(weights):
        block = dot(rows, weight[...]).astype(bf16)
        if scale is not None:
            block = (block.astype(f32) * scale).astype(bf16)
        pairs = weight.shape[1] // LANES
        for pair in range(pairs):
            target[side * pairs + pair] = block[:, pair * LANES : (pair + 1) * LANES]


def score_bound(query, key):
    row = lax.broadcasted_iota(jnp.int32, (LANES, LANES), 0) // HEAD_DIM
    col = lax.broadcasted_iota(jnp.int32, (LANES, LANES), 1) // HEAD_DIM
    same_head = jnp.where(row == col, 1.0, 0.0).astype(bf16)

    def longest(ref):
        most = None
        for pair in range(ref.shape[0]):
            x = ref[pair].astype(f32)
            found = jnp.max(dot((x * x).astype(bf16), same_head), axis=0, keepdims=True)
            most = found if most is None else jnp.maximum(most, found)
        return jnp.max(most)

    return longest(query) * longest(key) * 1.05


SAFE = 100.0


def attend(query, key, value, bias, block, finish, free=0):
    pairs, rows, _ = query.shape
    heads_at = lambda q, low, sub: jnp.where(low if sub == 0 else ~low, q, jnp.zeros_like(q))
    safe = score_bound(query, key) <= SAFE * SAFE

    def plain(pair, carry):
        k, v = key[pair], value[pair]
        low_v = low_lanes(v.shape)
        ones = jnp.ones_like(v)
        sides = [jnp.where(low_v, v, ones), jnp.where(low_v, ones, v)]
        for start in range(0, rows, block):
            at = slice(start, start + block)
            q = query[pair, at, :]
            low = low_lanes(q.shape)
            found = []
            for sub in range(2):
                s = lax.dot_general(heads_at(q, low, sub), k, ROWS_BY_ROWS, preferred_element_type=f32)
                p = jnp.exp2(s[:, free:] + bias[at, free:]).astype(bf16)
                if free:
                    p = jnp.concatenate([jnp.exp2(s[:, :free]).astype(bf16), p], 1)
                found.append(dot(p, sides[sub]))
            sums = pltpu.roll(jnp.where(low, found[1], found[0]), HEAD_DIM, 1)
            mixed = jnp.where(low, found[0], found[1]) * (1.0 / jnp.where(sums == 0.0, 1.0, sums))
            finish(pair, at, mixed, sums)
        return carry

    def careful(pair, carry):
        for start in range(0, rows, block):
            at = slice(start, start + block)
            q = query[pair, at, :]
            low = low_lanes(q.shape)
            mixes, sums = [], []
            for sub in range(2):
                s = lax.dot_general(
                    heads_at(q, low, sub), key[pair], ROWS_BY_ROWS, preferred_element_type=f32
                )
                p = jnp.exp2(s + bias[at, :])
                total = jnp.sum(p, -1, keepdims=True)
                w = (p * (1.0 / jnp.where(total == 0.0, 1.0, total))).astype(bf16)
                mixes.append(dot(w, value[pair]))
                sums.append(total)
            finish(pair, at, jnp.where(low, mixes[0], mixes[1]), jnp.where(low, sums[0], sums[1]))
        return carry

    @pl.when(safe)
    def _():
        lax.fori_loop(0, pairs, plain, 0)

    @pl.when(jnp.logical_not(safe))
    def _():
        lax.fori_loop(0, pairs, careful, 0)


def near_window_kernel(info, *refs):
    count = (len(refs) - 14) // 2
    nodes, weights = refs[: 2 * count], refs[2 * count : 2 * count + 6]
    query, mix, total, token, normed, key, value, bias = refs[2 * count + 6 :]
    lay(0, normed, nodes)
    rows = query.shape[1]
    project_pairs(query, normed[:rows, :], weights[:2], SCALE)
    project_pairs(key, normed[...], weights[2:4])
    project_pairs(value, normed[...], weights[4:])
    row = lax.broadcasted_iota(jnp.int32, bias.shape, 0)
    col = lax.broadcasted_iota(jnp.int32, bias.shape, 1)
    place = jnp.where(col < rows, col, col - rows + jnp.where(info[0] == 0, rows, -rows))
    bias[...] = jnp.where(jnp.abs(row - place) <= HALF_WIN, 0.0, NEGATIVE)
    token[...] = jnp.zeros_like(token)

    def finish(pair, at, mixed, sums):
        mix[pair, at, :] = mixed
        total[pair, at, :] = sums

    attend(query, key, value, bias, rows // 2, finish, free=rows)


def far_window_kernel(info, query, near_mix, near_total, *refs):
    count = len(refs) - 9
    nodes, weights = refs[:count], refs[count : count + 4]
    result, normed, key, value, bias = refs[count + 4 :]
    rows = query.shape[1]
    more = nodes[-1].shape[0]
    used = lay(0, normed, nodes)
    normed[used:, :] = jnp.zeros_like(normed[used:, :])
    project_pairs(key, normed[...], weights[:2])
    project_pairs(value, normed[...], weights[2:])
    first, whole, lead = info[1], info[2], info[0] == 0
    row = lax.broadcasted_iota(jnp.int32, bias.shape, 0)
    col = lax.broadcasted_iota(jnp.int32, bias.shape, 1)
    place = jnp.where(
        col < rows,
        col + jnp.where(lead, -rows, rows),
        jnp.where(
            col < rows + more,
            col - rows + jnp.where(lead, -rows - more, 2 * rows),
            col - rows - more + jnp.where(lead, 2 * rows, -rows - more),
        ),
    )
    live = (jnp.abs(row - place) <= HALF_WIN) & (first + place >= 0) & (first + place < whole) & (col < used)
    bias[...] = jnp.where(live, 0.0, NEGATIVE)

    def finish(pair, at, mixed, sums):
        near_sums = near_total[pair, at, :]
        inverse = 1.0 / (near_sums + sums)
        result[pair, at, :] = (near_mix[pair, at, :] * (near_sums * inverse) + mixed * (sums * inverse)).astype(bf16)

    attend(query, key, value, bias, rows, finish)


def feed_kernel(mix, mid, wo_mine, wo_other, up_mine, up_other, down_mine, down_other, result, passed, att, normed, total, *, start):
    index = pl.program_id(0)
    half = pl.num_programs(0) // 2

    @pl.when(index == 0)
    def _():
        pairs = wo_mine.shape[0] // LANES
        at = slice(start, start + result.shape[0])
        acc = mid[at, :].astype(f32)
        for side, wo in enumerate((wo_mine, wo_other)):
            block = jnp.concatenate([mix[side * pairs + pair, at, :] for pair in range(pairs)], 1)
            acc = acc + dot(block, wo[...])
        att[...] = acc.astype(bf16)
        normed[...] = layer_norm(att[...])
        total[...] = att[...].astype(f32)

    def part(up, down):
        inner = jax.nn.gelu(dot(normed[...], up[...]), approximate=True).astype(bf16)
        total[...] += dot(inner, down[...])

    @pl.when(index < half)
    def _():
        part(up_mine, down_mine)

    @pl.when(index >= half)
    def _():
        part(up_other, down_other)

    @pl.when(index == 2 * half - 1)
    def _():
        result[...] = total[...].astype(bf16)
        passed[...] = layer_norm(result[...])


def hold_kernel(*refs):
    del refs


POINTS = 32


def decoder_kernel(info, sources, counts, grid, *refs, spots):
    nodes_in, refs = refs[: len(spots)], refs[len(spots) :]
    wq_mine, wq_other, wo_mine, wo_other = refs[0], refs[1], refs[6], refs[7]
    result, table, query, product, gathered, weights, arrived, loaded = refs[8:]
    deep = query.shape[1]
    points = grid.shape[0]
    slots = sources.shape[0] // points
    piece = 256

    copies = [
        pltpu.make_async_copy(
            ref, gathered.at[pl.ds(pl.multiple_of(info[place] + offset, 16), ref.shape[0])], arrived.at[index]
        )
        for index, (ref, (place, offset)) in enumerate(zip(nodes_in, spots))
    ] + [pltpu.make_async_copy(ref, weights.at[index], loaded.at[index]) for index, ref in enumerate(refs[2:6])]
    for copy in copies:
        copy.start()
    count = gathered.shape[0] // 6

    def fill(index, carry):
        at = pl.ds(pl.multiple_of(index * count, 16), count)
        normed = gathered[at, :]
        for side in range(2):
            block = jnp.concatenate([dot(normed, weights[2 * side + half]) for half in range(2)], 1)
            table[at, side * deep : (side + 1) * deep, :] = block.reshape(count, deep, LANES)
        return carry

    def ask(index, carry):
        at = pl.ds(pl.multiple_of(index * piece, piece), piece)
        own_grid = grid[at, :]
        block = jnp.concatenate([dot(own_grid, weight[...]) for weight in (wq_mine, wq_other)], 1) * SCALE
        query[at] = block.reshape(piece, deep, LANES)
        return carry

    lax.fori_loop(0, points // piece, ask, 0)
    for copy in copies:
        copy.wait()
    lax.fori_loop(0, 6, fill, 0)

    ones_row = lax.broadcasted_iota(jnp.int32, (2 * LANES, 2 * LANES), 0) // HEAD_DIM
    ones_col = lax.broadcasted_iota(jnp.int32, (2 * LANES, 2 * LANES), 1) // HEAD_DIM
    same_head = jnp.where(ones_row == ones_col, 1.0, 0.0).astype(bf16)
    half = POINTS * deep // 2
    vectors = table.reshape(table.shape[0] * 2 * deep, LANES)

    def step(index, carry):
        first = index * POINTS
        for point in range(0, POINTS, 2):
            q = [query[first + point + t] for t in range(2)]
            for slot in range(slots):
                terms = []
                for t in range(2):
                    at = pl.multiple_of(sources[(first + point + t) * slots + slot], deep)
                    terms.append(vectors[pl.ds(at, deep), :] * q[t])
                product[slot, point * deep : (point + 2) * deep, :] = jnp.concatenate(terms, 0).astype(bf16)
        live = jnp.concatenate(
            [jnp.full((deep, LANES), counts[first + point], jnp.int32) for point in range(POINTS)], 0
        )
        powers = []
        for slot in range(slots):
            pair = jnp.concatenate([product[slot, :half, :], product[slot, half:, :]], 1)
            score = dot(pair, same_head)
            score = jnp.concatenate([score[:, :LANES], score[:, LANES:]], 0)
            powers.append(jnp.where(live > slot, jnp.exp2(score), 0.0))
        total = powers[0]
        for slot in range(1, slots):
            total = total + powers[slot]
        inverse = 1.0 / total
        weights = [p * inverse for p in powers]
        for point in range(POINTS):
            mixed = None
            for slot in range(slots):
                at = pl.multiple_of(sources[(first + point) * slots + slot], deep)
                term = weights[slot][point * deep : (point + 1) * deep, :] * vectors[pl.ds(at + deep, deep), :]
                mixed = term if mixed is None else mixed + term
            query[first + point] = mixed
        return carry

    lax.fori_loop(0, points // POINTS, step, 0)

    width = result.shape[0]
    inner = deep * LANES // 2

    def finish(index, carry):
        at = pl.ds(pl.multiple_of(index * piece, piece), piece)
        block = query[at].reshape(piece, deep * LANES).astype(bf16)
        acc = dot(block[:, :inner], wo_mine[...]) + dot(block[:, inner:], wo_other[...])
        result[:, at] = (grid[at, :].astype(f32) + acc).T[:width, :].astype(bf16)
        return carry

    lax.fori_loop(0, points // piece, finish, 0)


def local(
    grid_state,
    hidden_state,
    encoder_sources,
    encoder_counts,
    decoder_sources,
    decoder_counts,
    encoder_keys,
    encoder_values,
    encoder_query,
    encoder_output,
    window_query,
    window_keys,
    window_values,
    window_output,
    feed_up,
    feed_down,
    decoder_query,
    decoder_keys,
    decoder_values,
    decoder_output,
):
    bands, band, core = lax.axis_size("band"), lax.axis_index("band"), lax.axis_index("head")
    cores = lax.axis_size("head")
    grid_count, width = grid_state.shape
    nodes, channels = hidden_state.shape
    rows, points = nodes // cores, grid_count // cores
    full = channels * cores
    heads = full // HEAD_DIM

    def swap(x):
        return lax.ppermute(x, "head", [(0, 1), (1, 0)])

    def pair_swap(x):
        return lax.ppermute(x, "band", [(i, i ^ 1) for i in range(bands)])

    def pass_on(x):
        jumps = [(i, i + 2) for i in range(0, bands - 2, 2)] + [(i, i - 2) for i in range(3, bands, 2)]
        return lax.ppermute(x, "band", jumps)

    def my_part(x, size):
        return lax.dynamic_slice_in_dim(x, core * size, size, 0)

    def wide(x):
        return jnp.pad(x, ((0, LANES - x.shape[0]), (0, 0)))

    even = band % 2 == 0
    near_side = jnp.where(even, 2, 0)
    far_side = 2 - near_side
    info = jnp.stack(
        [
            core,
            band * nodes + core * rows,
            bands * nodes,
            near_side * grid_count + core * points,
            near_side * grid_count + (1 - core) * points,
            far_side * grid_count + core * points,
            far_side * grid_count + (1 - core) * points,
            nodes + core * rows,
            nodes + (1 - core) * rows,
            near_side * nodes + core * rows,
            near_side * nodes + (1 - core) * rows,
            far_side * nodes + core * rows,
            far_side * nodes + (1 - core) * rows,
        ]
    ).astype(jnp.int32)

    my_grid = my_part(grid_state, points)
    grid_cut = points // GRID_CHUNKS
    firsts = [pair_swap(my_grid[chunk * grid_cut : (chunk + 1) * grid_cut]) for chunk in range(GRID_CHUNKS)]

    kept = my_part(hidden_state, rows)
    got = swap(lax.dynamic_slice_in_dim(hidden_state, (1 - core) * rows, rows, 0))
    state = jnp.where(
        core == 0, jnp.concatenate([kept, got], 1), jnp.concatenate([got, kept], 1)
    )

    ek_mine, ev_mine, dq_mine = wide(encoder_keys), wide(encoder_values), wide(decoder_query)
    do_mine = jnp.pad(decoder_output, ((0, 0), (0, LANES - width)))

    my_sources = my_part(encoder_sources, rows).reshape(-1)
    my_counts = my_part(encoder_counts, rows)[:, None]
    dec_sources = ((my_part(decoder_sources, points) - (band - 1) * nodes) * (2 * full // LANES)).reshape(-1)
    dec_counts = my_part(decoder_counts, points)
    grid_wide = jnp.pad(my_grid, ((0, 0), (0, LANES - width)))
    early = (info, my_sources, my_counts)

    query, last = pl.pallas_call(
        query_kernel,
        out_shape=(
            jax.ShapeDtypeStruct((heads, rows, LANES), bf16),
            jax.ShapeDtypeStruct(firsts[-1].shape, bf16),
        ),
        in_specs=[VMEM] * 5 + [ANY] * (1 + len(early)),
        out_specs=(VMEM, ANY),
        input_output_aliases={5: 1},
        compiler_params=BIG,
        cost_estimate=cost(6 * rows * full * full),
        name="queries",
    )(state, encoder_query, swap(encoder_query), ek_mine, swap(ek_mine), firsts[-1], *early)

    grid_parts, grid_spots = [], []
    for chunk, first in enumerate(firsts[:-1] + [last]):
        second = pass_on(first)
        grid_parts += [first, swap(first), second, swap(second)]
        grid_spots += [(3 + side, chunk * grid_cut) for side in range(4)]

    slots = encoder_sources.shape[1]
    mid, normed_mid = pl.pallas_call(
        functools.partial(encoder_kernel, spots=tuple(grid_spots)),
        out_shape=(jax.ShapeDtypeStruct((rows, full), bf16),) * 2,
        in_specs=[SMEM, SMEM] + [VMEM] * (8 + len(grid_spots)),
        out_specs=(VMEM, VMEM),
        scratch_shapes=[pltpu.VMEM((3 * grid_count, LANES), f32)]
        + [pltpu.VMEM((GROUP * slots, LANES), f32) for _ in range(CHAINS)]
        + [pltpu.VMEM((heads, rows, LANES), f32)],
        compiler_params=BIG,
        cost_estimate=cost(16 * rows * full * full),
        name="encoder",
    )(
        info, my_sources, my_counts, query, grid_state, *grid_parts,
        ev_mine, swap(ev_mine), encoder_output, swap(encoder_output), state,
    )

    more = HALF_WIN - rows
    facing = [(2 * i + 1, 2 * i + 2) for i in range(bands - 1)]
    facing = facing + [(b, a) for a, b in facing]
    partner = swap(normed_mid)
    edge = jnp.where(core == 0, partner[:more], partner[rows - more :])
    far = lax.ppermute(jnp.concatenate([normed_mid, edge], 0), ("band", "head"), facing)

    pairs = full // LANES
    window_weights = (window_keys, swap(window_keys), window_values, swap(window_values))
    near_count = 2 * rows
    win_query, near_mix, near_sum, token = pl.pallas_call(
        near_window_kernel,
        out_shape=(
            jax.ShapeDtypeStruct((pairs, rows, LANES), bf16),
            jax.ShapeDtypeStruct((pairs, rows, LANES), f32),
            jax.ShapeDtypeStruct((pairs, rows, LANES), f32),
            jax.ShapeDtypeStruct((8, LANES), jnp.int32),
        ),
        in_specs=[SMEM] + [VMEM] * 8,
        out_specs=(VMEM,) * 4,
        scratch_shapes=[
            pltpu.VMEM((near_count, full), bf16),
            pltpu.VMEM((pairs, near_count, LANES), bf16),
            pltpu.VMEM((pairs, near_count, LANES), bf16),
            pltpu.VMEM((rows, near_count), f32),
        ],
        compiler_params=BIG,
        cost_estimate=cost(1024),
        name="near_window",
    )(info, normed_mid, partner, window_query, swap(window_query), *window_weights)

    near = swap(
        jnp.where(core + token[0, 0] == 0, far[rows - more : rows], far[:more])
    )
    far_count = -(-(rows + 2 * more) // LANES) * LANES
    mix = pl.pallas_call(
        far_window_kernel,
        out_shape=jax.ShapeDtypeStruct((pairs, rows, LANES), bf16),
        in_specs=[SMEM] + [VMEM] * 9,
        out_specs=VMEM,
        scratch_shapes=[
            pltpu.VMEM((far_count, full), bf16),
            pltpu.VMEM((pairs, far_count, LANES), bf16),
            pltpu.VMEM((pairs, far_count, LANES), bf16),
            pltpu.VMEM((rows, far_count), f32),
        ],
        compiler_params=BIG,
        cost_estimate=cost(20 * rows * full * full),
        name="far_window",
    )(info, win_query, near_mix, near_sum, far, near, *window_weights)

    units = feed_up.shape[1]
    chunk = min(512, units)
    steps = units // chunk
    whole = lambda shape: pl.BlockSpec(shape, lambda i: (0,) * len(shape))
    cuts = (rows * 5 // 8, rows - rows * 5 // 8)
    weights = (
        window_output, swap(window_output), feed_up, swap(feed_up), feed_down, swap(feed_down),
    )

    def feed(start, cut):
        return pl.pallas_call(
            functools.partial(feed_kernel, start=start),
            grid=(2 * steps,),
            out_shape=(jax.ShapeDtypeStruct((cut, full), bf16),) * 2,
            in_specs=[
                whole((pairs, rows, LANES)),
                whole((rows, full)),
                whole((channels, full)),
                whole((channels, full)),
                pl.BlockSpec((full, chunk), lambda i: (0, jnp.minimum(i, steps - 1))),
                pl.BlockSpec((full, chunk), lambda i: (0, jnp.maximum(i - steps, 0))),
                pl.BlockSpec((chunk, full), lambda i: (jnp.minimum(i, steps - 1), 0)),
                pl.BlockSpec((chunk, full), lambda i: (jnp.maximum(i - steps, 0), 0)),
            ],
            out_specs=(whole((cut, full)),) * 2,
            scratch_shapes=[
                pltpu.VMEM((cut, full), bf16),
                pltpu.VMEM((cut, full), bf16),
                pltpu.VMEM((cut, full), f32),
            ],
            compiler_params=BIG,
            cost_estimate=cost(2 * cut * full * (full + 4 * units)),
            name="feed",
        )(mix, mid, *weights)

    node_parts, node_spots, own_parts, partner_parts = [], [], [], []
    firsts, seconds = [], []
    for index, cut in enumerate(cuts):
        start = sum(cuts[:index])
        final, normed = feed(start, cut)
        first = pair_swap(normed)
        firsts.append(first)
        if index < len(cuts) - 1:
            seconds.append(pass_on(first))
        own_parts.append(lax.dynamic_slice_in_dim(final, core * channels, channels, 1))
        partner_parts.append(swap(lax.dynamic_slice_in_dim(final, (1 - core) * channels, channels, 1)))
        node_parts += [normed, swap(normed)]
        node_spots += [(7 + side, start) for side in range(2)]

    deep = full // LANES
    decoder_weights = (decoder_keys, swap(decoder_keys), decoder_values, swap(decoder_values))

    own_columns, partner_columns = jnp.concatenate(own_parts, 0), jnp.concatenate(partner_parts, 0)
    hidden_final = jnp.where(
        core == 0,
        jnp.concatenate([own_columns, partner_columns], 0),
        jnp.concatenate([partner_columns, own_columns], 0),
    )

    dec_slots = decoder_sources.shape[1]
    firsts[-1] = pl.pallas_call(
        hold_kernel,
        out_shape=jax.ShapeDtypeStruct(firsts[-1].shape, bf16),
        in_specs=[ANY] * 4,
        out_specs=ANY,
        input_output_aliases={0: 0},
        name="hold",
    )(firsts[-1], dec_sources, dec_counts, grid_wide)
    for index, first in enumerate(firsts):
        second = pass_on(first) if index == len(cuts) - 1 else seconds[index]
        node_parts += [first, swap(first), second, swap(second)]
        node_spots += [(9 + side, sum(cuts[:index])) for side in range(4)]

    grid_next = pl.pallas_call(
        functools.partial(decoder_kernel, spots=tuple(node_spots)),
        out_shape=jax.ShapeDtypeStruct((width, points), bf16),
        in_specs=[SMEM] * 3 + [VMEM] + [ANY] * len(node_spots) + [VMEM] * 2 + [ANY] * 4 + [VMEM] * 2,
        out_specs=VMEM,
        scratch_shapes=[
            pltpu.VMEM((3 * nodes, 2 * deep, LANES), f32),
            pltpu.VMEM((points, deep, LANES), f32),
            pltpu.VMEM((dec_slots, POINTS * deep, LANES), bf16),
            pltpu.VMEM((3 * nodes, full), bf16),
            pltpu.VMEM((4,) + decoder_keys.shape, bf16),
            pltpu.SemaphoreType.DMA((len(node_spots),)),
            pltpu.SemaphoreType.DMA((4,)),
        ],
        compiler_params=BIG,
        name="decoder",
    )(
        info, dec_sources, dec_counts, grid_wide, *node_parts,
        dq_mine, swap(dq_mine), *decoder_weights,
        do_mine, swap(do_mine),
    )
    return (grid_next.T, hidden_final)


def solution(mesh):
    in_specs = (
        P("band", None),
        P("band", "head"),
        P("band", None),
        P("band"),
        P("band", None),
        P("band"),
        P(None, "head"),
        P(None, "head"),
        P(None, "head"),
        P("head", None),
        P(None, "head"),
        P(None, "head"),
        P(None, "head"),
        P("head", None),
        P(None, "head"),
        P("head", None),
        P(None, "head"),
        P(None, "head"),
        P(None, "head"),
        P("head", None),
    )
    out_specs = (P(("band", "head"), None), P("band", "head"))
    return jax.shard_map(local, mesh=mesh, in_specs=in_specs, out_specs=out_specs, check_vma=False)
```

```python
import functools
import math

import jax
import jax.numpy as jnp
from jax import lax
from jax.experimental import pallas as pl
from jax.experimental.pallas import tpu as pltpu
from jax.sharding import PartitionSpec as P

HALF_WIN = 560
HEAD_DIM = 64
LANES = 128
EPSILON = 1e-05
NEGATIVE = -1e30
SCALE = HEAD_DIM ** (-0.5) * math.log2(math.e)

bf16 = jnp.bfloat16
f32 = jnp.float32
ROWS_BY_ROWS = (((1,), (1,)), ((), ()))
VMEM = pl.BlockSpec(memory_space=pltpu.VMEM)
SMEM = pl.BlockSpec(memory_space=pltpu.SMEM)
ANY = pl.BlockSpec(memory_space=pl.ANY)
BIG = pltpu.CompilerParams(vmem_limit_bytes=58 * 2**20)


def cost(flops):
    return pl.CostEstimate(flops=flops, bytes_accessed=flops // 256, transcendentals=0)


def dot(a, b):
    return jnp.dot(a, b, preferred_element_type=f32)


def layer_norm(matrix):
    x = matrix.astype(f32)
    centred = x - jnp.mean(x, axis=-1, keepdims=True)
    variance = jnp.mean(centred * centred, axis=-1, keepdims=True)
    return (centred * lax.rsqrt(variance + EPSILON)).astype(bf16)


def low_lanes(shape):
    return lax.broadcasted_iota(jnp.int32, shape, len(shape) - 1) % LANES < HEAD_DIM


def query_kernel(state, wq_mine, wq_other, keys_mine, keys_other, passing, *refs):
    out, passed = refs[-2:]
    del passing, passed
    normed = layer_norm(state[...])
    pairs = wq_mine.shape[1] // LANES
    for side, (wq, keys) in enumerate(((wq_mine, keys_mine), (wq_other, keys_other))):
        query = (dot(normed, wq[...])).astype(bf16)
        for pair in range(pairs):
            two = query[:, pair * LANES : (pair + 1) * LANES]
            low = low_lanes(two.shape)
            weight = keys[:, pair * LANES : (pair + 1) * LANES]
            for sub in range(2):
                one = jnp.where(low if sub == 0 else ~low, two, jnp.zeros_like(two))
                out[(side * pairs + pair) * 2 + sub] = (
                    lax.dot_general(one, weight, ROWS_BY_ROWS, preferred_element_type=f32) * SCALE
                ).astype(bf16)


GRID_CHUNKS = 2
GROUP = 8
CHAINS = 16


def encoder_kernel(
    info, sources, counts, query, own, *refs, spots,
):
    near, refs = refs[: len(spots)], refs[len(spots) :]
    values_mine, values_other, out_mine, out_other, state, result, normed, table = refs[:8]
    picked, mix = refs[8:-1], refs[-1]
    grid_count, width = own.shape
    heads = query.shape[0]
    rows = result.shape[0]
    slots = sources.shape[0] // query.shape[1]
    span = GROUP * slots
    table[...] = jnp.zeros_like(table)

    def fill(start, ref):
        table[pl.ds(pl.multiple_of(start, 8), ref.shape[0]), :width] = ref[...].astype(f32)

    fill(grid_count, own)
    for ref, (place, offset) in zip(near, spots):
        fill(info[place] + offset, ref)

    node = lax.broadcasted_iota(jnp.int32, (GROUP, span), 0)
    slot = lax.broadcasted_iota(jnp.int32, (GROUP, span), 1) - node * slots

    def step(index, carry):
        groups = [index * CHAINS + chain for chain in range(CHAINS)]
        starts = [pl.multiple_of(group * GROUP, GROUP) for group in groups]
        for group, rows_ref in zip(groups, picked):
            base = group * span
            for s in range(span):
                rows_ref[s : s + 1, :] = table[pl.ds(sources[base + s], 1), :]
        grids = [ref[...].astype(bf16) for ref in picked]
        live = [(slot >= 0) & (slot < counts[pl.ds(start, GROUP), :]) for start in starts]
        asked = query[:, pl.ds(pl.multiple_of(index * (CHAINS * GROUP), 16), CHAINS * GROUP), :].astype(f32)
        queries = [
            asked[:, chain * GROUP : (chain + 1) * GROUP, :].reshape(heads * GROUP, LANES).astype(bf16)
            for chain in range(CHAINS)
        ]
        scores = [
            lax.dot_general(q, g, ROWS_BY_ROWS, preferred_element_type=f32)
            for q, g in zip(queries, grids)
        ]
        powers = [
            jnp.where(on[None], jnp.exp2(s.reshape(heads, GROUP, span)), 0.0).reshape(
                heads * GROUP, span
            )
            for s, on in zip(scores, live)
        ]
        weights = [(p * (1.0 / jnp.sum(p, -1, keepdims=True))).astype(bf16) for p in powers]
        mixed = [dot(w, g) for w, g in zip(weights, grids)]
        for start, m in zip(starts, mixed):
            mix[:, pl.ds(start, GROUP), :] = m.reshape(heads, GROUP, LANES)
        return carry

    lax.fori_loop(0, rows // (GROUP * CHAINS), step, 0)

    pairs = values_mine.shape[1] // LANES
    total = state[...].astype(f32)
    for side, (values, out) in enumerate(((values_mine, out_mine), (values_other, out_other))):
        parts = []
        for pair in range(pairs):
            weight = values[:, pair * LANES : (pair + 1) * LANES]
            low = low_lanes(weight.shape)
            both = jnp.concatenate(
                [jnp.where(low, weight, 0.0).astype(bf16), jnp.where(low, 0.0, weight).astype(bf16)], 0
            )
            head = (side * pairs + pair) * 2
            two = jnp.concatenate([mix[head].astype(bf16), mix[head + 1].astype(bf16)], 1)
            parts.append(dot(two, both).astype(bf16))
        total = total + dot(jnp.concatenate(parts, 1), out[...])
    result[...] = total.astype(bf16)
    normed[...] = layer_norm(result[...])


def lay(start, block, refs):
    for ref in refs:
        block[start : start + ref.shape[0], :] = ref[...]
        start += ref.shape[0]
    return start


def project_pairs(target, rows, weights, scale=None):
    for side, weight in enumerate(weights):
        block = dot(rows, weight[...]).astype(bf16)
        if scale is not None:
            block = (block.astype(f32) * scale).astype(bf16)
        pairs = weight.shape[1] // LANES
        for pair in range(pairs):
            target[side * pairs + pair] = block[:, pair * LANES : (pair + 1) * LANES]


def score_bound(query, key):
    row = lax.broadcasted_iota(jnp.int32, (LANES, LANES), 0) // HEAD_DIM
    col = lax.broadcasted_iota(jnp.int32, (LANES, LANES), 1) // HEAD_DIM
    same_head = jnp.where(row == col, 1.0, 0.0).astype(bf16)

    def longest(ref):
        most = None
        for pair in range(ref.shape[0]):
            x = ref[pair].astype(f32)
            found = jnp.max(dot((x * x).astype(bf16), same_head), axis=0, keepdims=True)
            most = found if most is None else jnp.maximum(most, found)
        return jnp.max(most)

    return longest(query) * longest(key) * 1.05


SAFE = 100.0


def attend(query, key, value, bias, block, finish, free=0):
    pairs, rows, _ = query.shape
    heads_at = lambda q, low, sub: jnp.where(low if sub == 0 else ~low, q, jnp.zeros_like(q))
    safe = score_bound(query, key) <= SAFE * SAFE

    def plain(pair, carry):
        k, v = key[pair], value[pair]
        low_v = low_lanes(v.shape)
        ones = jnp.ones_like(v)
        sides = [jnp.where(low_v, v, ones), jnp.where(low_v, ones, v)]
        for start in range(0, rows, block):
            at = slice(start, start + block)
            q = query[pair, at, :]
            low = low_lanes(q.shape)
            found = []
            for sub in range(2):
                s = lax.dot_general(heads_at(q, low, sub), k, ROWS_BY_ROWS, preferred_element_type=f32)
                p = jnp.exp2(s[:, free:] + bias[at, free:]).astype(bf16)
                if free:
                    p = jnp.concatenate([jnp.exp2(s[:, :free]).astype(bf16), p], 1)
                found.append(dot(p, sides[sub]))
            sums = pltpu.roll(jnp.where(low, found[1], found[0]), HEAD_DIM, 1)
            mixed = jnp.where(low, found[0], found[1]) * (1.0 / jnp.where(sums == 0.0, 1.0, sums))
            finish(pair, at, mixed, sums)
        return carry

    def careful(pair, carry):
        for start in range(0, rows, block):
            at = slice(start, start + block)
            q = query[pair, at, :]
            low = low_lanes(q.shape)
            mixes, sums = [], []
            for sub in range(2):
                s = lax.dot_general(
                    heads_at(q, low, sub), key[pair], ROWS_BY_ROWS, preferred_element_type=f32
                )
                p = jnp.exp2(s + bias[at, :])
                total = jnp.sum(p, -1, keepdims=True)
                w = (p * (1.0 / jnp.where(total == 0.0, 1.0, total))).astype(bf16)
                mixes.append(dot(w, value[pair]))
                sums.append(total)
            finish(pair, at, jnp.where(low, mixes[0], mixes[1]), jnp.where(low, sums[0], sums[1]))
        return carry

    @pl.when(safe)
    def _():
        lax.fori_loop(0, pairs, plain, 0)

    @pl.when(jnp.logical_not(safe))
    def _():
        lax.fori_loop(0, pairs, careful, 0)


def near_window_kernel(info, *refs):
    count = (len(refs) - 14) // 2
    nodes, weights = refs[: 2 * count], refs[2 * count : 2 * count + 6]
    query, mix, total, token, normed, key, value, bias = refs[2 * count + 6 :]
    lay(0, normed, nodes)
    rows = query.shape[1]
    project_pairs(query, normed[:rows, :], weights[:2], SCALE)
    project_pairs(key, normed[...], weights[2:4])
    project_pairs(value, normed[...], weights[4:])
    row = lax.broadcasted_iota(jnp.int32, bias.shape, 0)
    col = lax.broadcasted_iota(jnp.int32, bias.shape, 1)
    place = jnp.where(col < rows, col, col - rows + jnp.where(info[0] == 0, rows, -rows))
    bias[...] = jnp.where(jnp.abs(row - place) <= HALF_WIN, 0.0, NEGATIVE)
    token[...] = jnp.zeros_like(token)

    def finish(pair, at, mixed, sums):
        mix[pair, at, :] = mixed
        total[pair, at, :] = sums

    attend(query, key, value, bias, rows // 2, finish, free=rows)


def far_window_kernel(info, query, near_mix, near_total, *refs):
    count = len(refs) - 9
    nodes, weights = refs[:count], refs[count : count + 4]
    result, normed, key, value, bias = refs[count + 4 :]
    rows = query.shape[1]
    more = nodes[-1].shape[0]
    used = lay(0, normed, nodes)
    normed[used:, :] = jnp.zeros_like(normed[used:, :])
    project_pairs(key, normed[...], weights[:2])
    project_pairs(value, normed[...], weights[2:])
    first, whole, lead = info[1], info[2], info[0] == 0
    row = lax.broadcasted_iota(jnp.int32, bias.shape, 0)
    col = lax.broadcasted_iota(jnp.int32, bias.shape, 1)
    place = jnp.where(
        col < rows,
        col + jnp.where(lead, -rows, rows),
        jnp.where(
            col < rows + more,
            col - rows + jnp.where(lead, -rows - more, 2 * rows),
            col - rows - more + jnp.where(lead, 2 * rows, -rows - more),
        ),
    )
    live = (jnp.abs(row - place) <= HALF_WIN) & (first + place >= 0) & (first + place < whole) & (col < used)
    bias[...] = jnp.where(live, 0.0, NEGATIVE)

    def finish(pair, at, mixed, sums):
        near_sums = near_total[pair, at, :]
        inverse = 1.0 / (near_sums + sums)
        result[pair, at, :] = (near_mix[pair, at, :] * (near_sums * inverse) + mixed * (sums * inverse)).astype(bf16)

    attend(query, key, value, bias, rows, finish)


def feed_kernel(mix, mid, wo_mine, wo_other, up_mine, up_other, down_mine, down_other, result, passed, att, normed, total, *, start):
    index = pl.program_id(0)
    half = pl.num_programs(0) // 2

    @pl.when(index == 0)
    def _():
        pairs = wo_mine.shape[0] // LANES
        at = slice(start, start + result.shape[0])
        acc = mid[at, :].astype(f32)
        for side, wo in enumerate((wo_mine, wo_other)):
            block = jnp.concatenate([mix[side * pairs + pair, at, :] for pair in range(pairs)], 1)
            acc = acc + dot(block, wo[...])
        att[...] = acc.astype(bf16)
        normed[...] = layer_norm(att[...])
        total[...] = att[...].astype(f32)

    def part(up, down):
        inner = jax.nn.gelu(dot(normed[...], up[...]), approximate=True).astype(bf16)
        total[...] += dot(inner, down[...])

    @pl.when(index < half)
    def _():
        part(up_mine, down_mine)

    @pl.when(index >= half)
    def _():
        part(up_other, down_other)

    @pl.when(index == 2 * half - 1)
    def _():
        result[...] = total[...].astype(bf16)
        passed[...] = layer_norm(result[...])


def hold_kernel(*refs):
    del refs


POINTS = 32


def decoder_kernel(info, sources, counts, grid, *refs, spots):
    nodes_in, refs = refs[: len(spots)], refs[len(spots) :]
    wq_mine, wq_other, wo_mine, wo_other = refs[0], refs[1], refs[6], refs[7]
    result, table, query, product, gathered, weights, arrived, loaded = refs[8:]
    deep = query.shape[1]
    points = grid.shape[0]
    slots = sources.shape[0] // points
    piece = 256

    copies = [
        pltpu.make_async_copy(
            ref, gathered.at[pl.ds(pl.multiple_of(info[place] + offset, 16), ref.shape[0])], arrived.at[index]
        )
        for index, (ref, (place, offset)) in enumerate(zip(nodes_in, spots))
    ] + [pltpu.make_async_copy(ref, weights.at[index], loaded.at[index]) for index, ref in enumerate(refs[2:6])]
    for copy in copies:
        copy.start()
    count = gathered.shape[0] // 6

    def fill(index, carry):
        at = pl.ds(pl.multiple_of(index * count, 16), count)
        normed = gathered[at, :]
        for side in range(2):
            block = jnp.concatenate([dot(normed, weights[2 * side + half]) for half in range(2)], 1)
            table[at, side * deep : (side + 1) * deep, :] = block.reshape(count, deep, LANES)
        return carry

    def ask(index, carry):
        at = pl.ds(pl.multiple_of(index * piece, piece), piece)
        own_grid = grid[at, :]
        block = jnp.concatenate([dot(own_grid, weight[...]) for weight in (wq_mine, wq_other)], 1) * SCALE
        query[at] = block.reshape(piece, deep, LANES)
        return carry

    lax.fori_loop(0, points // piece, ask, 0)
    for copy in copies:
        copy.wait()
    lax.fori_loop(0, 6, fill, 0)

    ones_row = lax.broadcasted_iota(jnp.int32, (2 * LANES, 2 * LANES), 0) // HEAD_DIM
    ones_col = lax.broadcasted_iota(jnp.int32, (2 * LANES, 2 * LANES), 1) // HEAD_DIM
    same_head = jnp.where(ones_row == ones_col, 1.0, 0.0).astype(bf16)
    half = POINTS * deep // 2
    vectors = table.reshape(table.shape[0] * 2 * deep, LANES)

    def step(index, carry):
        first = index * POINTS
        for point in range(0, POINTS, 2):
            q = [query[first + point + t] for t in range(2)]
            for slot in range(slots):
                terms = []
                for t in range(2):
                    at = pl.multiple_of(sources[(first + point + t) * slots + slot], deep)
                    terms.append(vectors[pl.ds(at, deep), :] * q[t])
                product[slot, point * deep : (point + 2) * deep, :] = jnp.concatenate(terms, 0).astype(bf16)
        live = jnp.concatenate(
            [jnp.full((deep, LANES), counts[first + point], jnp.int32) for point in range(POINTS)], 0
        )
        powers = []
        for slot in range(slots):
            pair = jnp.concatenate([product[slot, :half, :], product[slot, half:, :]], 1)
            score = dot(pair, same_head)
            score = jnp.concatenate([score[:, :LANES], score[:, LANES:]], 0)
            powers.append(jnp.where(live > slot, jnp.exp2(score), 0.0))
        total = powers[0]
        for slot in range(1, slots):
            total = total + powers[slot]
        inverse = 1.0 / total
        weights = [p * inverse for p in powers]
        for point in range(POINTS):
            mixed = None
            for slot in range(slots):
                at = pl.multiple_of(sources[(first + point) * slots + slot], deep)
                term = weights[slot][point * deep : (point + 1) * deep, :] * vectors[pl.ds(at + deep, deep), :]
                mixed = term if mixed is None else mixed + term
            query[first + point] = mixed
        return carry

    lax.fori_loop(0, points // POINTS, step, 0)

    width = result.shape[0]
    inner = deep * LANES // 2

    def finish(index, carry):
        at = pl.ds(pl.multiple_of(index * piece, piece), piece)
        block = query[at].reshape(piece, deep * LANES).astype(bf16)
        acc = dot(block[:, :inner], wo_mine[...]) + dot(block[:, inner:], wo_other[...])
        result[:, at] = (grid[at, :].astype(f32) + acc).T[:width, :].astype(bf16)
        return carry

    lax.fori_loop(0, points // piece, finish, 0)


def local(
    grid_state,
    hidden_state,
    encoder_sources,
    encoder_counts,
    decoder_sources,
    decoder_counts,
    encoder_keys,
    encoder_values,
    encoder_query,
    encoder_output,
    window_query,
    window_keys,
    window_values,
    window_output,
    feed_up,
    feed_down,
    decoder_query,
    decoder_keys,
    decoder_values,
    decoder_output,
):
    bands, band, core = lax.axis_size("band"), lax.axis_index("band"), lax.axis_index("head")
    cores = lax.axis_size("head")
    grid_count, width = grid_state.shape
    nodes, channels = hidden_state.shape
    rows, points = nodes // cores, grid_count // cores
    full = channels * cores
    heads = full // HEAD_DIM

    def swap(x):
        return lax.ppermute(x, "head", [(0, 1), (1, 0)])

    def pair_swap(x):
        return lax.ppermute(x, "band", [(i, i ^ 1) for i in range(bands)])

    def pass_on(x):
        jumps = [(i, i + 2) for i in range(0, bands - 2, 2)] + [(i, i - 2) for i in range(3, bands, 2)]
        return lax.ppermute(x, "band", jumps)

    def my_part(x, size):
        return lax.dynamic_slice_in_dim(x, core * size, size, 0)

    def wide(x):
        return jnp.pad(x, ((0, LANES - x.shape[0]), (0, 0)))

    even = band % 2 == 0
    near_side = jnp.where(even, 2, 0)
    far_side = 2 - near_side
    info = jnp.stack(
        [
            core,
            band * nodes + core * rows,
            bands * nodes,
            near_side * grid_count + core * points,
            near_side * grid_count + (1 - core) * points,
            far_side * grid_count + core * points,
            far_side * grid_count + (1 - core) * points,
            nodes + core * rows,
            nodes + (1 - core) * rows,
            near_side * nodes + core * rows,
            near_side * nodes + (1 - core) * rows,
            far_side * nodes + core * rows,
            far_side * nodes + (1 - core) * rows,
        ]
    ).astype(jnp.int32)

    my_grid = my_part(grid_state, points)
    grid_cut = points // GRID_CHUNKS
    firsts = [pair_swap(my_grid[chunk * grid_cut : (chunk + 1) * grid_cut]) for chunk in range(GRID_CHUNKS)]

    kept = my_part(hidden_state, rows)
    got = swap(lax.dynamic_slice_in_dim(hidden_state, (1 - core) * rows, rows, 0))
    state = jnp.where(
        core == 0, jnp.concatenate([kept, got], 1), jnp.concatenate([got, kept], 1)
    )

    ek_mine, ev_mine, dq_mine = wide(encoder_keys), wide(encoder_values), wide(decoder_query)
    do_mine = jnp.pad(decoder_output, ((0, 0), (0, LANES - width)))

    my_sources = my_part(encoder_sources, rows).reshape(-1)
    my_counts = my_part(encoder_counts, rows)[:, None]
    dec_sources = ((my_part(decoder_sources, points) - (band - 1) * nodes) * (2 * full // LANES)).reshape(-1)
    dec_counts = my_part(decoder_counts, points)
    grid_wide = jnp.pad(my_grid, ((0, 0), (0, LANES - width)))
    early = (info, my_sources, my_counts)

    query, last = pl.pallas_call(
        query_kernel,
        out_shape=(
            jax.ShapeDtypeStruct((heads, rows, LANES), bf16),
            jax.ShapeDtypeStruct(firsts[-1].shape, bf16),
        ),
        in_specs=[VMEM] * 5 + [ANY] * (1 + len(early)),
        out_specs=(VMEM, ANY),
        input_output_aliases={5: 1},
        compiler_params=BIG,
        cost_estimate=cost(6 * rows * full * full),
        name="queries",
    )(state, encoder_query, swap(encoder_query), ek_mine, swap(ek_mine), firsts[-1], *early)

    grid_parts, grid_spots = [], []
    for chunk, first in enumerate(firsts[:-1] + [last]):
        second = pass_on(first)
        grid_parts += [first, swap(first), second, swap(second)]
        grid_spots += [(3 + side, chunk * grid_cut) for side in range(4)]

    slots = encoder_sources.shape[1]
    mid, normed_mid = pl.pallas_call(
        functools.partial(encoder_kernel, spots=tuple(grid_spots)),
        out_shape=(jax.ShapeDtypeStruct((rows, full), bf16),) * 2,
        in_specs=[SMEM, SMEM] + [VMEM] * (8 + len(grid_spots)),
        out_specs=(VMEM, VMEM),
        scratch_shapes=[pltpu.VMEM((3 * grid_count, LANES), f32)]
        + [pltpu.VMEM((GROUP * slots, LANES), f32) for _ in range(CHAINS)]
        + [pltpu.VMEM((heads, rows, LANES), f32)],
        compiler_params=BIG,
        cost_estimate=cost(16 * rows * full * full),
        name="encoder",
    )(
        info, my_sources, my_counts, query, grid_state, *grid_parts,
        ev_mine, swap(ev_mine), encoder_output, swap(encoder_output), state,
    )

    more = HALF_WIN - rows
    facing = [(2 * i + 1, 2 * i + 2) for i in range(bands - 1)]
    facing = facing + [(b, a) for a, b in facing]
    partner = swap(normed_mid)
    edge = jnp.where(core == 0, partner[:more], partner[rows - more :])
    far = lax.ppermute(jnp.concatenate([normed_mid, edge], 0), ("band", "head"), facing)

    pairs = full // LANES
    window_weights = (window_keys, swap(window_keys), window_values, swap(window_values))
    near_count = 2 * rows
    win_query, near_mix, near_sum, token = pl.pallas_call(
        near_window_kernel,
        out_shape=(
            jax.ShapeDtypeStruct((pairs, rows, LANES), bf16),
            jax.ShapeDtypeStruct((pairs, rows, LANES), f32),
            jax.ShapeDtypeStruct((pairs, rows, LANES), f32),
            jax.ShapeDtypeStruct((8, LANES), jnp.int32),
        ),
        in_specs=[SMEM] + [VMEM] * 8,
        out_specs=(VMEM,) * 4,
        scratch_shapes=[
            pltpu.VMEM((near_count, full), bf16),
            pltpu.VMEM((pairs, near_count, LANES), bf16),
            pltpu.VMEM((pairs, near_count, LANES), bf16),
            pltpu.VMEM((rows, near_count), f32),
        ],
        compiler_params=BIG,
        cost_estimate=cost(1024),
        name="near_window",
    )(info, normed_mid, partner, window_query, swap(window_query), *window_weights)

    near = swap(
        jnp.where(core + token[0, 0] == 0, far[rows - more : rows], far[:more])
    )
    far_count = -(-(rows + 2 * more) // LANES) * LANES
    mix = pl.pallas_call(
        far_window_kernel,
        out_shape=jax.ShapeDtypeStruct((pairs, rows, LANES), bf16),
        in_specs=[SMEM] + [VMEM] * 9,
        out_specs=VMEM,
        scratch_shapes=[
            pltpu.VMEM((far_count, full), bf16),
            pltpu.VMEM((pairs, far_count, LANES), bf16),
            pltpu.VMEM((pairs, far_count, LANES), bf16),
            pltpu.VMEM((rows, far_count), f32),
        ],
        compiler_params=BIG,
        cost_estimate=cost(20 * rows * full * full),
        name="far_window",
    )(info, win_query, near_mix, near_sum, far, near, *window_weights)

    units = feed_up.shape[1]
    chunk = min(512, units)
    steps = units // chunk
    whole = lambda shape: pl.BlockSpec(shape, lambda i: (0,) * len(shape))
    cuts = (rows * 5 // 8, rows - rows * 5 // 8)
    weights = (
        window_output, swap(window_output), feed_up, swap(feed_up), feed_down, swap(feed_down),
    )

    def feed(start, cut):
        return pl.pallas_call(
            functools.partial(feed_kernel, start=start),
            grid=(2 * steps,),
            out_shape=(jax.ShapeDtypeStruct((cut, full), bf16),) * 2,
            in_specs=[
                whole((pairs, rows, LANES)),
                whole((rows, full)),
                whole((channels, full)),
                whole((channels, full)),
                pl.BlockSpec((full, chunk), lambda i: (0, jnp.minimum(i, steps - 1))),
                pl.BlockSpec((full, chunk), lambda i: (0, jnp.maximum(i - steps, 0))),
                pl.BlockSpec((chunk, full), lambda i: (jnp.minimum(i, steps - 1), 0)),
                pl.BlockSpec((chunk, full), lambda i: (jnp.maximum(i - steps, 0), 0)),
            ],
            out_specs=(whole((cut, full)),) * 2,
            scratch_shapes=[
                pltpu.VMEM((cut, full), bf16),
                pltpu.VMEM((cut, full), bf16),
                pltpu.VMEM((cut, full), f32),
            ],
            compiler_params=BIG,
            cost_estimate=cost(2 * cut * full * (full + 4 * units)),
            name="feed",
        )(mix, mid, *weights)

    node_parts, node_spots, own_parts, partner_parts = [], [], [], []
    firsts, seconds = [], []
    for index, cut in enumerate(cuts):
        start = sum(cuts[:index])
        final, normed = feed(start, cut)
        first = pair_swap(normed)
        firsts.append(first)
        if index < len(cuts) - 1:
            seconds.append(pass_on(first))
        own_parts.append(lax.dynamic_slice_in_dim(final, core * channels, channels, 1))
        partner_parts.append(swap(lax.dynamic_slice_in_dim(final, (1 - core) * channels, channels, 1)))
        node_parts += [normed, swap(normed)]
        node_spots += [(7 + side, start) for side in range(2)]

    deep = full // LANES
    decoder_weights = (decoder_keys, swap(decoder_keys), decoder_values, swap(decoder_values))

    own_columns, partner_columns = jnp.concatenate(own_parts, 0), jnp.concatenate(partner_parts, 0)
    hidden_final = jnp.where(
        core == 0,
        jnp.concatenate([own_columns, partner_columns], 0),
        jnp.concatenate([partner_columns, own_columns], 0),
    )

    dec_slots = decoder_sources.shape[1]
    firsts[-1] = pl.pallas_call(
        hold_kernel,
        out_shape=jax.ShapeDtypeStruct(firsts[-1].shape, bf16),
        in_specs=[ANY] * 4,
        out_specs=ANY,
        input_output_aliases={0: 0},
        name="hold",
    )(firsts[-1], dec_sources, dec_counts, grid_wide)
    for index, first in enumerate(firsts):
        second = pass_on(first) if index == len(cuts) - 1 else seconds[index]
        node_parts += [first, swap(first), second, swap(second)]
        node_spots += [(9 + side, sum(cuts[:index])) for side in range(4)]

    grid_next = pl.pallas_call(
        functools.partial(decoder_kernel, spots=tuple(node_spots)),
        out_shape=jax.ShapeDtypeStruct((width, points), bf16),
        in_specs=[SMEM] * 3 + [VMEM] + [ANY] * len(node_spots) + [VMEM] * 2 + [ANY] * 4 + [VMEM] * 2,
        out_specs=VMEM,
        scratch_shapes=[
            pltpu.VMEM((3 * nodes, 2 * deep, LANES), f32),
            pltpu.VMEM((points, deep, LANES), f32),
            pltpu.VMEM((dec_slots, POINTS * deep, LANES), bf16),
            pltpu.VMEM((3 * nodes, full), bf16),
            pltpu.VMEM((4,) + decoder_keys.shape, bf16),
            pltpu.SemaphoreType.DMA((len(node_spots),)),
            pltpu.SemaphoreType.DMA((4,)),
        ],
        compiler_params=BIG,
        name="decoder",
    )(
        info, dec_sources, dec_counts, grid_wide, *node_parts,
        dq_mine, swap(dq_mine), *decoder_weights,
        do_mine, swap(do_mine),
    )
    return (grid_next.T, hidden_final)


def solution(mesh):
    in_specs = (
        P("band", None),
        P("band", "head"),
        P("band", None),
        P("band"),
        P("band", None),
        P("band"),
        P(None, "head"),
        P(None, "head"),
        P(None, "head"),
        P("head", None),
        P(None, "head"),
        P(None, "head"),
        P(None, "head"),
        P("head", None),
        P(None, "head"),
        P("head", None),
        P(None, "head"),
        P(None, "head"),
        P(None, "head"),
        P("head", None),
    )
    out_specs = (P(("band", "head"), None), P("band", "head"))
    return jax.shard_map(local, mesh=mesh, in_specs=in_specs, out_specs=out_specs, check_vma=False)
```
